512 devices in a mesh: section: 16 (over z), expert: 32 (over y, x, core).
Axes of the slice: x: 4, y: 4, z: 16, core: 2. Of those that a mesh axis runs over, the one named last changes fastest.
Arguments:
- fwd_in: bfloat16 [16, 256, 3584], P('section', 'expert'), may hold values from -6 to 6
- fwd_enter: bfloat16 [1, 256, 3584], P(None, 'expert'), may hold values from -6 to 6
- bwd_in: bfloat16 [16, 256, 3584], P('section', 'expert'), may hold values from -6 to 6
- bwd_enter: bfloat16 [1, 256, 3584], P(None, 'expert'), may hold values from -6 to 6
- saved: bfloat16 [16, 2, 256, 3584], P('section', None, 'expert'), may hold values from -6 to 6
- fwd_routes: int32 [16, 2, 256, 2], P('section'), may hold values from 0 to 3, all different within a row; in each aligned block of 8 rows (0 to 7, 8 to 15, ..., all dimensions but the last counted through in order) at most 6 rows name the same one
- fwd_gates: float32 [16, 2, 256, 2], P('section'), may hold values from 0.2 to 1
- bwd_routes: int32 [16, 2, 256, 2], P('section'), may hold values from 0 to 3, all different within a row; in each aligned block of 8 rows (0 to 7, 8 to 15, ..., all dimensions but the last counted through in order) at most 6 rows name the same one
- bwd_gates: float32 [16, 2, 256, 2], P('section'), may hold values from 0.2 to 1
- gain: float32 [16, 3584], P('section'), may hold values from 0.5 to 1.5
- w_gate: bfloat16 [16, 3584, 4096], P('section', None, 'expert'), may hold values from -0.09375 to 0.09375
- w_up: bfloat16 [16, 3584, 4096], P('section', None, 'expert'), may hold values from -0.09375 to 0.09375
- w_down: bfloat16 [16, 4096, 3584], P('section', 'expert'), may hold values from -0.1875 to 0.1875
Outputs:
- fwd_out: bfloat16 [16, 2, 256, 3584], P('section', None, 'expert')
- bwd_out: bfloat16 [16, 2, 256, 3584], P('section', None, 'expert')
The draws below stay inside these ranges and needn't reach their ends.
Inputs may be any that keep to these rules, and one draw needn't show every extreme that they name: `fwd_routes`: in each aligned block of 8 rows (the tokens of one device) a row names 2 different experts and no expert is named by more than 6 rows; some expert is named by exactly 6 rows in some block. `bwd_routes`: in each aligned block of 8 rows (the tokens of one device) a row names 2 different experts and no expert is named by more than 6 rows; some expert is named by exactly 6 rows in some block.
All inputs are finite; a program needn't handle non-finite values.
Results may differ from the reference program's by a relative error of at most 0.0095.
Values may be sent and summed in bfloat16 or wider, within the bound.
A program may use at most 64 MiB of HBM per device.

```python
import math
import jax
import jax.numpy as jnp
import numpy as np
from jax import lax

D = 3584
FF_DEV = 128
EXPERTS = 4
TOP = 2
STEPS = 2
TOK_DEV = 8
CAP = 6
FF = 1024
TOKENS = 256
N_SECTION = 16
N_EXPERT = 32


def block_scale(rng, shape, split, least, largest):
    factor_of = 1.0
    for dim, shards_of in split:
        heights = jax.random.uniform(jax.random.fold_in(jax.random.fold_in(rng, 6), dim), (shards_of,), jnp.float32, least / len(split), largest / len(split))
        factor_of = factor_of * jnp.repeat(jnp.exp(heights), shape[dim] // shards_of).reshape((-1,) + (1,) * (len(shape) - 1 - dim))
    return factor_of


def routed_block(key, own, number, rows, number_of, top, limit, slope):
    sequence = jax.random.permutation(key, number_of)
    crowded, usual = portions_of(number_of, rows * top, limit, slope, True), portions_of(number_of, rows * top, limit, slope, False)
    places = jnp.arange(number_of)

    def named(lengths, turn):
        used = int((lengths > 0).sum())
        fixed = max(1, used // 4)
        moved = fixed + (places - fixed + turn * (used - fixed)) % max(1, number_of - fixed)
        return jnp.zeros((number_of,), jnp.int32).at[sequence[jnp.where(places < fixed, places, moved)]].set(jnp.asarray(lengths, jnp.int32))

    lengths = jnp.where(number % 4 == 0, named(crowded, number // 4), named(usual, number - number // 4 - 1))
    mixed = jax.random.permutation(jax.random.fold_in(own, 3), number_of)
    source_of, receiver = mixed[0:number_of // 2 * 2:2], mixed[1:number_of // 2 * 2:2]
    slack = jnp.minimum(lengths[source_of] - 1, limit - lengths[receiver]) // 2
    slack = jnp.where((source_of == sequence[0]) | (receiver == sequence[0]) | (lengths[receiver] == 0), 0, jnp.maximum(slack, 0))
    moved = jax.random.randint(jax.random.fold_in(own, 4), (number_of // 2,), 0, 1 << 20) % (slack + 1)
    lengths = lengths.at[source_of].add(-moved).at[receiver].add(moved)
    members = jnp.searchsorted(jnp.cumsum(lengths), jnp.arange(rows * top), side="right").astype(jnp.int32)
    grid = members.reshape(top, rows).T
    grid = grid[jax.random.permutation(jax.random.fold_in(own, 1), rows)]
    turn = jax.random.randint(jax.random.fold_in(own, 2), (rows, 1), 0, top)
    return jnp.take_along_axis(grid, (jnp.arange(top)[None, :] + turn) % top, axis=1)


def portions_of(number_of, total, reach, skew, full):
    loads = [(1 << 20) // math.isqrt(rank ** skew) + 1 for rank in range(1, number_of + 1)]
    largest = reach if full else min(reach, max(-(-total // number_of), total * loads[0] // sum(loads)))
    least = 1 if total - largest >= number_of - 1 else 0
    holding, rest = [largest] + [least] * (number_of - 1), total - largest - least * (number_of - 1)
    while rest > 0:
        candidates = [i for i in range(1, number_of) if holding[i] < largest] or [i for i in range(1, number_of) if holding[i] < reach]
        mass, left = sum([loads[i] for i in candidates]), rest
        for i in candidates:
            addition = min(reach - holding[i], max(1, left * loads[i] // mass), rest)
            holding[i] = holding[i] + addition
            rest = rest - addition
    return np.array(holding)


def noise(own_key, shape, scale, reach, split=(), held_as=jnp.bfloat16):
    array = scale * jax.random.normal(own_key, shape, jnp.float32)
    if split:
        array = array * block_scale(own_key, shape, split, -0.22, 0.18)
    return jnp.clip(array, -reach, reach).astype(held_as)


def setup_inputs(seed: int = 0) -> dict:
    key_of = jax.random.split(jax.random.key(seed), 14)
    fwd_in = noise(key_of[0], (N_SECTION, TOKENS, D), 1.0, 6.0, ((0, 16), (1, 32)))
    fwd_enter = noise(key_of[1], (STEPS - 1, TOKENS, D), 1.0, 6.0, ((1, 32),))
    bwd_in = noise(key_of[2], (N_SECTION, TOKENS, D), 1.0, 6.0, ((0, 16), (1, 32)))
    bwd_enter = noise(key_of[3], (STEPS - 1, TOKENS, D), 1.0, 6.0, ((1, 32),))
    saved = noise(key_of[4], (N_SECTION, STEPS, TOKENS, D), 1.0, 6.0, ((0, 16), (2, 32)))
    fwd_routes_keys = jax.random.split(jax.random.fold_in(key_of[5], 1), N_SECTION * STEPS * TOKENS // TOK_DEV)
    fwd_routes_turns = jax.random.permutation(jax.random.fold_in(key_of[5], 3), N_SECTION * STEPS * TOKENS // TOK_DEV)
    fwd_routes = jax.vmap(lambda own, number: routed_block(jax.random.fold_in(key_of[5], 2), own, number, TOK_DEV, EXPERTS, TOP, CAP, 2))(fwd_routes_keys, fwd_routes_turns).reshape((N_SECTION, STEPS, TOKENS, TOP))
    fwd_gates = jnp.clip(0.2 + 0.8 * jax.random.uniform(key_of[6], (N_SECTION, STEPS, TOKENS, TOP), jnp.float32) ** block_scale(key_of[6], (N_SECTION, STEPS, TOKENS, TOP), ((0, 16),), -0.2, 0.2), 0.2, 1.0)
    bwd_routes_keys = jax.random.split(jax.random.fold_in(key_of[7], 1), N_SECTION * STEPS * TOKENS // TOK_DEV)
    bwd_routes_turns = jax.random.permutation(jax.random.fold_in(key_of[7], 3), N_SECTION * STEPS * TOKENS // TOK_DEV)
    bwd_routes = jax.vmap(lambda own, number: routed_block(jax.random.fold_in(key_of[7], 2), own, number, TOK_DEV, EXPERTS, TOP, CAP, 2))(bwd_routes_keys, bwd_routes_turns).reshape((N_SECTION, STEPS, TOKENS, TOP))
    bwd_gates = jnp.clip(0.2 + 0.8 * jax.random.uniform(key_of[8], (N_SECTION, STEPS, TOKENS, TOP), jnp.float32) ** block_scale(key_of[8], (N_SECTION, STEPS, TOKENS, TOP), ((0, 16),), -0.2, 0.2), 0.2, 1.0)
    gain = jnp.clip(1.0 + 0.1 * jax.random.normal(key_of[9], (N_SECTION, D), jnp.float32), 0.5, 1.5)
    w_gate = noise(key_of[10], (N_SECTION, D, EXPERTS * FF), D ** -0.5, 0.09375, ((0, 16), (2, 32)))
    w_up = noise(key_of[11], (N_SECTION, D, EXPERTS * FF), D ** -0.5, 0.09375, ((0, 16), (2, 32)))
    w_down = noise(key_of[12], (N_SECTION, EXPERTS * FF, D), FF ** -0.5, 0.1875, ((0, 16), (1, 32)))
    return dict(fwd_in=fwd_in, fwd_enter=fwd_enter, bwd_in=bwd_in, bwd_enter=bwd_enter, saved=saved, fwd_routes=fwd_routes, fwd_gates=fwd_gates, bwd_routes=bwd_routes, bwd_gates=bwd_gates, gain=gain, w_gate=w_gate, w_up=w_up, w_down=w_down)


EPSILON = 1e-06

def normalize(inputs, scale_gain):
    scale = lax.rsqrt(lax.optimization_barrier(jnp.mean(inputs * inputs, axis=-1, keepdims=True)) + EPSILON)
    return (scale, (inputs * scale * scale_gain).astype(jnp.bfloat16))

def layer_forward(block, routes, gates, scale_gain, w_gate, w_up, w_down):
    inputs = block.astype(jnp.float32)
    scale, normed = normalize(inputs, scale_gain)
    groups = N_EXPERT // EXPERTS
    width = w_gate.shape[1] // EXPERTS
    count = inputs.shape[0]
    total = jnp.zeros(inputs.shape, jnp.float32)
    for expert in range(EXPERTS):
        factor = lax.optimization_barrier(jnp.sum(jnp.where(routes == expert, gates, jnp.zeros_like(gates)), axis=-1))
        start = expert * width
        gate_pre = jnp.dot(normed, w_gate[:, start:start + width], preferred_element_type=jnp.float32)
        up_pre = jnp.dot(normed, w_up[:, start:start + width], preferred_element_type=jnp.float32)
        hidden = (jax.nn.silu(gate_pre) * up_pre).astype(jnp.bfloat16)
        pieces = jnp.einsum('tsf,sfd->tsd', hidden.reshape(count, groups, FF_DEV).astype(jnp.float32), w_down[start:start + width].reshape(groups, FF_DEV, D).astype(jnp.float32))
        rounded = lax.optimization_barrier(pieces.astype(jnp.bfloat16))
        total = total + factor[:, None] * lax.optimization_barrier(jnp.sum(rounded.astype(jnp.float32), axis=1))
    return (inputs + total).astype(jnp.bfloat16)

def layer_backward(block, upstream_in, routes, gates, scale_gain, w_gate, w_up, w_down):
    inputs = block.astype(jnp.float32)
    upstream = upstream_in.astype(jnp.float32)
    scale, normed = normalize(inputs, scale_gain)
    groups = N_EXPERT // EXPERTS
    width = w_gate.shape[1] // EXPERTS
    count = inputs.shape[0]
    total = jnp.zeros(inputs.shape, jnp.float32)
    for expert in range(EXPERTS):
        factor = lax.optimization_barrier(jnp.sum(jnp.where(routes == expert, gates, jnp.zeros_like(gates)), axis=-1))
        start = expert * width
        grads = (factor[:, None] * upstream).astype(jnp.bfloat16)
        gate_pre = jnp.dot(normed, w_gate[:, start:start + width], preferred_element_type=jnp.float32)
        up_pre = jnp.dot(normed, w_up[:, start:start + width], preferred_element_type=jnp.float32)
        sigma = jax.nn.sigmoid(gate_pre)
        d_hidden = jnp.dot(grads, w_down[start:start + width].T, preferred_element_type=jnp.float32)
        d_gate = (d_hidden * up_pre * sigma * (1.0 + gate_pre * (1.0 - sigma))).astype(jnp.bfloat16)
        d_up = (d_hidden * gate_pre * sigma).astype(jnp.bfloat16)
        gate_cols = w_gate[:, start:start + width].reshape(D, groups, FF_DEV).astype(jnp.float32)
        up_cols = w_up[:, start:start + width].reshape(D, groups, FF_DEV).astype(jnp.float32)
        pieces = jnp.einsum('tsf,dsf->tsd', d_gate.reshape(count, groups, FF_DEV).astype(jnp.float32), gate_cols)
        pieces = pieces + jnp.einsum('tsf,dsf->tsd', d_up.reshape(count, groups, FF_DEV).astype(jnp.float32), up_cols)
        rounded = lax.optimization_barrier(pieces.astype(jnp.bfloat16))
        total = total + lax.optimization_barrier(jnp.sum(rounded.astype(jnp.float32), axis=1))
    product = total * scale_gain
    change = scale * product - inputs * scale ** 3 * lax.optimization_barrier(jnp.mean(product * inputs, axis=-1, keepdims=True))
    return (upstream + change).astype(jnp.bfloat16)

def reference(fwd_in, fwd_enter, bwd_in, bwd_enter, saved, fwd_routes, fwd_gates, bwd_routes, bwd_gates, gain, w_gate, w_up, w_down):
    carry_forward = fwd_in
    carry_backward = bwd_in
    forward_list = []
    backward_list = []
    for step in range(STEPS):
        outputs = lax.map(lambda packed: layer_forward(*packed), (carry_forward, fwd_routes[:, step], fwd_gates[:, step], gain, w_gate, w_up, w_down))
        grads = lax.map(lambda packed: layer_backward(*packed), (saved[:, step], carry_backward, bwd_routes[:, step], bwd_gates[:, step], gain, w_gate, w_up, w_down))
        forward_list.append(outputs)
        backward_list.append(grads)
        if step + 1 < STEPS:
            carry_forward = jnp.concatenate([fwd_enter[step][None], outputs[:-1]], axis=0)
            carry_backward = jnp.concatenate([grads[1:], bwd_enter[step][None]], axis=0)
    return (jnp.stack(forward_list, axis=1), jnp.stack(backward_list, axis=1))
```

```python
import functools

import jax
import jax.numpy as jnp
from jax import lax
from jax.experimental import pallas as pl
from jax.experimental.pallas import tpu as pltpu
from jax.sharding import PartitionSpec as P

EPSILON = 1e-06
MESH = pl.DeviceIdType.MESH
SIDE = 4
CORES = 2
PEERS = (1, 2, 3)
TILE = 512
F32 = jnp.float32
BF16 = jnp.bfloat16


def normalize(inputs, gain):
    scale = lax.rsqrt(jnp.mean(inputs * inputs, axis=-1, keepdims=True) + EPSILON)
    return scale, (inputs * scale * gain).astype(BF16)


def relay_kernel(
    sections,
    fwd_in,
    fwd_enter,
    bwd_in,
    bwd_enter,
    saved,
    fwd_routes,
    fwd_gates,
    bwd_routes,
    bwd_gates,
    gain,
    w_gate,
    w_up,
    w_down,
    fwd_out,
    bwd_out,
    in_f,
    enter_f,
    in_b,
    enter_b,
    in_s,
    routes_f,
    gates_f,
    routes_b,
    gates_b,
    gain_v,
    w_in,
    w_back,
    gathered,
    partial,
    landed_one,
    middle,
    landed_two,
    hop_send,
    hop_land,
    pre_act,
    load_sem,
    weight_send,
    weight_recv,
    gather_send,
    gather_recv,
    reduce_send,
    reduce_recv,
    hop_send_sem,
    hop_recv_sem,
):
    width = gain.shape[-1]
    half = width // 2
    unit = w_down.shape[0]
    rows = in_f.shape[0]
    tokens = SIDE * SIDE * rows
    section = lax.axis_index("section")
    place = lax.axis_index("expert")
    core = lax.rem(place, CORES)
    x = lax.rem(place // CORES, SIDE)
    y = place // (CORES * SIDE)

    def device(dy=0, dx=0, dc=0, dz=0):
        at_y, at_x = lax.rem(y + dy, SIDE), lax.rem(x + dx, SIDE)
        at_c = lax.rem(core + dc, CORES)
        return (lax.rem(section + dz, sections), (at_y * SIDE + at_x) * CORES + at_c)

    sibling = device(dc=1)
    following, preceding = device(dz=1), device(dz=sections - 1)
    along_y = [device(dy=k) for k in PEERS]
    along_x = [device(dx=k) for k in PEERS]

    barrier = pltpu.get_barrier_semaphore()
    greeted = [sibling, following, preceding] + along_y + along_x
    for other in greeted:
        pl.semaphore_signal(barrier, inc=1, device_id=other, device_id_type=MESH)

    small = [
        (fwd_in.at[0], in_f),
        (gain, gain_v),
        (saved.at[0], in_s),
        (bwd_in.at[0], in_b),
        (fwd_routes, routes_f),
        (fwd_gates, gates_f),
        (bwd_routes, routes_b),
        (bwd_gates, gates_b),
        (fwd_enter.at[0], enter_f),
        (bwd_enter.at[0], enter_b),
    ]
    own_weights = [
        (w_gate, w_in.at[:, pl.ds(0, unit)]),
        (w_up, w_in.at[:, pl.ds(2 * unit, unit)]),
        (w_down, w_back.at[pl.ds(0, unit), :]),
    ]
    sibling_weights = [
        (w_gate, w_in.at[:, pl.ds(unit, unit)]),
        (w_up, w_in.at[:, pl.ds(3 * unit, unit)]),
        (w_down, w_back.at[pl.ds(unit, unit), :]),
    ]
    loads = [
        pltpu.make_async_copy(source, target, load_sem.at[i])
        for i, (source, target) in enumerate(small + own_weights)
    ]
    for load in loads:
        load.start()
    for load in loads[: len(small)]:
        load.wait()

    gain_row = gain_v[...]
    block = (x, y)
    _, normed = normalize(in_f[...].astype(F32), gain_row)
    gathered[0, x, y] = normed
    scales = []
    for step in range(2):
        scale, normed = normalize(in_s[step].astype(F32), gain_row)
        scales.append(scale)
        gathered[1 + 3 * step, x, y] = normed
    gathered[2, x, y] = in_b[...]

    pl.semaphore_wait(barrier, len(greeted))

    first, second = pl.ds(0, half), pl.ds(half, half)

    def gather_one(u):
        out = []
        for k in range(len(PEERS)):
            for part, (peers, columns) in enumerate(((along_y, first), (along_x, second))):
                spot = gathered.at[u, x, y, :, columns]
                out.append(remote(spot, spot, gather_send, gather_recv, (u, 0, part, k), peers[k]))
        return out

    def gather_two(u):
        out = []
        for k in range(len(PEERS)):
            spot = gathered.at[u, x, :, :, first]
            out.append(remote(spot, spot, gather_send, gather_recv, (u, 1, 0, k), along_x[k]))
            spot = gathered.at[u, :, y, :, second]
            out.append(remote(spot, spot, gather_send, gather_recv, (u, 1, 1, k), along_y[k]))
        return out

    def remote(source, target, send, recv, index, other):
        return pltpu.make_async_remote_copy(
            src_ref=source,
            dst_ref=target,
            send_sem=send.at[index],
            recv_sem=recv.at[index],
            device_id=other,
            device_id_type=MESH,
        )

    def reduce_one(u):
        out = []
        for k, step in enumerate(PEERS):
            at_x, at_y = lax.rem(x + step, SIDE), lax.rem(y + step, SIDE)
            out.append(
                remote(
                    partial.at[u, at_x, :, :, first],
                    landed_one.at[u, 0, k],
                    reduce_send,
                    reduce_recv,
                    (u, 0, 0, k),
                    along_x[k],
                )
            )
            out.append(
                remote(
                    partial.at[u, :, at_y, :, second],
                    landed_one.at[u, 1, k],
                    reduce_send,
                    reduce_recv,
                    (u, 0, 1, k),
                    along_y[k],
                )
            )
        return out

    def reduce_middle(u):
        own = (partial[u, x, :, :, :half], partial[u, :, y, :, half:])
        for part in range(2):
            total = own[part].astype(F32)
            for k in range(len(PEERS)):
                total = total + landed_one[u, part, k].astype(F32)
            middle[u, part] = total.astype(BF16)

    def reduce_two(u):
        out = []
        for k, step in enumerate(PEERS):
            at_x, at_y = lax.rem(x + step, SIDE), lax.rem(y + step, SIDE)
            for part, (at, peers) in enumerate(((at_y, along_y), (at_x, along_x))):
                out.append(
                    remote(
                        middle.at[u, part, at],
                        landed_two.at[u, part, k],
                        reduce_send,
                        reduce_recv,
                        (u, 1, part, k),
                        peers[k],
                    )
                )
        return out

    def reduce_end(u):
        sums = []
        for part, at in enumerate((y, x)):
            total = middle[u, part, at].astype(F32)
            for k in range(len(PEERS)):
                total = total + landed_two[u, part, k].astype(F32)
            sums.append(total)
        return jnp.concatenate(sums, axis=-1)

    sent = []

    def start(copies):
        for copy in copies:
            copy.start()
        sent.extend(copies)
        return copies

    def arrive(copies):
        for copy in copies:
            copy.wait_recv()

    own_tokens = lax.broadcasted_iota(jnp.int32, (tokens, 1), 0)
    col = own_tokens // (SIDE * rows)
    row = lax.rem(own_tokens // rows, SIDE)
    wanted = ((row * SIDE + col) * CORES + core) * rows + lax.rem(own_tokens, rows)

    def factor(routes, gates, step):
        chosen = jnp.where(routes[step] == y, gates[step], 0.0)
        line = jnp.sum(chosen, axis=0, keepdims=True)
        lanes = lax.broadcasted_iota(jnp.int32, (tokens, line.shape[-1]), 1)
        return jnp.sum(jnp.where(lanes == wanted, line, 0.0), axis=-1, keepdims=True)

    def tile_of(u, columns):
        return gathered[u, :, :, :, columns].reshape(tokens, TILE)

    tiles = width // TILE

    def pre_activation(u):
        def body(i, total):
            columns = pl.ds(pl.multiple_of(i * TILE, TILE), TILE)
            return total + jnp.dot(
                tile_of(u, columns), w_in[columns, :], preferred_element_type=F32
            )

        return lax.fori_loop(0, tiles, body, jnp.zeros((tokens, 4 * unit), F32))

    def forward(u, target, factor_column):
        both = pre_activation(u)
        a, up = both[:, : 2 * unit], both[:, 2 * unit :]
        hidden = (a / (1.0 + jnp.exp(-a)) * up).astype(BF16)

        @pl.loop(0, tiles)
        def _(i):
            columns = pl.ds(pl.multiple_of(i * TILE, TILE), TILE)
            piece = jnp.dot(hidden, w_back[:, columns], preferred_element_type=F32)
            partial[target, :, :, :, columns] = (
                (piece * factor_column).astype(BF16).reshape(SIDE, SIDE, rows, TILE)
            )

    contract = (((1,), (1,)), ((), ()))

    def backward(u, target, both, factor_column):
        a, up = both[:, : 2 * unit], both[:, 2 * unit :]

        def body(i, total):
            columns = pl.ds(pl.multiple_of(i * TILE, TILE), TILE)
            return total + lax.dot_general(
                tile_of(u, columns), w_back[:, columns], contract, preferred_element_type=F32
            )

        d_hidden = lax.fori_loop(0, tiles, body, jnp.zeros((tokens, 2 * unit), F32))
        d_hidden = d_hidden * factor_column
        sigma = 1.0 / (1.0 + jnp.exp(-a))
        d_gate = (d_hidden * up * sigma * (1.0 + a * (1.0 - sigma))).astype(BF16)
        d_up = (d_hidden * a * sigma).astype(BF16)
        grads = jnp.concatenate([d_gate, d_up], axis=-1)

        @pl.loop(0, tiles)
        def _(i):
            columns = pl.ds(pl.multiple_of(i * TILE, TILE), TILE)
            piece = lax.dot_general(
                grads, w_in[columns, :], contract, preferred_element_type=F32
            )
            partial[target, :, :, :, columns] = piece.astype(BF16).reshape(
                SIDE, SIDE, rows, TILE
            )

    def forward_end(u, inputs):
        return (inputs.astype(F32) + reduce_end(u)).astype(BF16)

    def backward_end(u, step, upstream):
        inputs = in_s[step].astype(F32)
        scale = scales[step]
        product = reduce_end(u) * gain_row
        change = scale * product - inputs * scale**3 * jnp.mean(
            product * inputs, axis=-1, keepdims=True
        )
        return (upstream.astype(F32) + change).astype(BF16)

    gather_f = start(gather_one(0))
    weights = []
    for i, (source, target) in enumerate(sibling_weights):
        weights.append(
            pltpu.make_async_remote_copy(
                src_ref=source,
                dst_ref=target,
                send_sem=weight_send.at[i],
                recv_sem=weight_recv.at[i],
                device_id=sibling,
                device_id_type=MESH,
            )
        )
    start(weights)
    gather_s = start(gather_one(1))
    gather_g = start(gather_one(2))
    factors_f = [factor(routes_f, gates_f, step) for step in range(2)]
    factors_b = [factor(routes_b, gates_b, step) for step in range(2)]
    arrive(gather_f)
    gather_f = start(gather_two(0))
    arrive(gather_s)
    gather_s = start(gather_two(1))
    arrive(gather_g)
    gather_g = start(gather_two(2))
    for load in loads[len(small) :]:
        load.wait()
    arrive(weights)
    arrive(gather_f)
    forward(0, 0, factors_f[0])
    reduce_f = start(reduce_one(0))
    arrive(gather_s)
    both = pre_activation(1)
    arrive(gather_g)
    backward(2, 1, both, factors_b[0])
    reduce_b = start(reduce_one(1))
    gather_s = start(gather_one(4))
    arrive(reduce_f)
    reduce_middle(0)
    reduce_f = start(reduce_two(0))
    arrive(reduce_b)
    reduce_middle(1)
    reduce_b = start(reduce_two(1))
    arrive(gather_s)
    gather_s = start(gather_two(4))
    arrive(reduce_f)
    outputs = forward_end(0, in_f[...])
    hop_send[0] = outputs
    hop_f = start([remote(hop_send.at[0], hop_land.at[0], hop_send_sem, hop_recv_sem, (0,), following)])
    fwd_out[0, 0] = outputs
    arrive(reduce_b)
    outputs = backward_end(1, 0, in_b[...])
    hop_send[1] = outputs
    hop_b = start([remote(hop_send.at[1], hop_land.at[1], hop_send_sem, hop_recv_sem, (1,), preceding)])
    bwd_out[0, 0] = outputs

    arrive(hop_f)
    moved_f = jnp.where(section == 0, enter_f[...].astype(F32), hop_land[0].astype(F32))
    _, normed = normalize(moved_f, gain_row)
    gathered[3, x, y] = normed
    gather_f = start(gather_one(3))
    arrive(hop_b)
    moved_b = jnp.where(
        section == sections - 1, enter_b[...].astype(F32), hop_land[1].astype(F32)
    ).astype(BF16)
    gathered[5, x, y] = moved_b
    gather_g = start(gather_one(5))
    arrive(gather_s)
    pre_act[...] = pre_activation(4)
    arrive(gather_f)
    gather_f = start(gather_two(3))
    arrive(gather_g)
    gather_g = start(gather_two(5))
    arrive(gather_f)
    forward(3, 2, factors_f[1])
    reduce_f = start(reduce_one(2))
    arrive(gather_g)
    backward(5, 3, pre_act[...], factors_b[1])
    reduce_b = start(reduce_one(3))
    arrive(reduce_f)
    reduce_middle(2)
    reduce_f = start(reduce_two(2))
    arrive(reduce_b)
    reduce_middle(3)
    reduce_b = start(reduce_two(3))
    arrive(reduce_f)
    fwd_out[0, 1] = forward_end(2, moved_f)
    arrive(reduce_b)
    bwd_out[0, 1] = backward_end(3, 1, moved_b)
    for copy in sent:
        copy.wait_send()


def per_device(
    fwd_in,
    fwd_enter,
    bwd_in,
    bwd_enter,
    saved,
    fwd_routes,
    fwd_gates,
    bwd_routes,
    bwd_gates,
    gain,
    w_gate,
    w_up,
    w_down,
):
    sections = lax.axis_size("section")
    steps, rows, width = saved.shape[1:]
    unit = w_gate.shape[-1]
    half = width // 2
    peers = len(PEERS)
    turned = [
        jnp.transpose(array[0], (0, 2, 1)) for array in (fwd_routes, fwd_gates, bwd_routes, bwd_gates)
    ]
    in_hbm = pl.BlockSpec(memory_space=pltpu.HBM)
    in_vmem = pl.BlockSpec(memory_space=pltpu.VMEM)
    table = turned[0].shape
    dma = pltpu.SemaphoreType.DMA
    scratch = [
        pltpu.VMEM((rows, width), BF16),
        pltpu.VMEM((rows, width), BF16),
        pltpu.VMEM((rows, width), BF16),
        pltpu.VMEM((rows, width), BF16),
        pltpu.VMEM((steps, rows, width), BF16),
        pltpu.VMEM(table, jnp.int32),
        pltpu.VMEM(table, F32),
        pltpu.VMEM(table, jnp.int32),
        pltpu.VMEM(table, F32),
        pltpu.VMEM((1, width), F32),
        pltpu.VMEM((width, 4 * unit), BF16),
        pltpu.VMEM((2 * unit, width), BF16),
        pltpu.VMEM((6, SIDE, SIDE, rows, width), BF16),
        pltpu.VMEM((4, SIDE, SIDE, rows, width), BF16),
        pltpu.VMEM((4, 2, peers, SIDE, rows, half), BF16),
        pltpu.VMEM((4, 2, SIDE, rows, half), BF16),
        pltpu.VMEM((4, 2, peers, rows, half), BF16),
        pltpu.VMEM((2, rows, width), BF16),
        pltpu.VMEM((2, rows, width), BF16),
        pltpu.VMEM((SIDE * SIDE * rows, 4 * unit), F32),
        dma((13,)),
        dma((3,)),
        dma((3,)),
        dma((6, 2, 2, peers)),
        dma((6, 2, 2, peers)),
        dma((4, 2, 2, peers)),
        dma((4, 2, 2, peers)),
        dma((2,)),
        dma((2,)),
    ]
    out = jax.ShapeDtypeStruct((1, steps, rows, width), BF16)
    return pl.pallas_call(
        functools.partial(relay_kernel, sections),
        out_shape=(out, out),
        in_specs=[in_hbm] * 13,
        out_specs=(in_vmem, in_vmem),
        scratch_shapes=scratch,
        compiler_params=pltpu.CompilerParams(
            collective_id=0, has_side_effects=True, vmem_limit_bytes=60 * 2**20
        ),
        name="relay",
    )(
        fwd_in,
        fwd_enter,
        bwd_in,
        bwd_enter,
        saved,
        *turned,
        gain,
        w_gate[0],
        w_up[0],
        w_down[0],
    )


def solution(mesh):
    in_specs = (
        P("section", "expert", None),
        P(None, "expert", None),
        P("section", "expert", None),
        P(None, "expert", None),
        P("section", None, "expert", None),
        P("section", None, None, None),
        P("section", None, None, None),
        P("section", None, None, None),
        P("section", None, None, None),
        P("section", None),
        P("section", None, "expert"),
        P("section", None, "expert"),
        P("section", "expert", None),
    )
    out_specs = (P("section", None, "expert", None), P("section", None, "expert", None))
    return jax.shard_map(
        per_device, mesh=mesh, in_specs=in_specs, out_specs=out_specs, check_vma=False
    )
```

```python
import functools

import jax
import jax.numpy as jnp
from jax import lax
from jax.experimental import pallas as pl
from jax.experimental.pallas import tpu as pltpu
from jax.sharding import PartitionSpec as P

EPSILON = 1e-06
MESH = pl.DeviceIdType.MESH
SIDE = 4
CORES = 2
PEERS = (1, 2, 3)
CAP = 6
F32 = jnp.float32
BF16 = jnp.bfloat16


def normalize(inputs, gain):
    scale = lax.rsqrt(jnp.mean(inputs * inputs, axis=-1, keepdims=True) + EPSILON)
    return scale, (inputs * scale * gain).astype(BF16)


def relay_kernel(
    sections,
    fwd_in,
    fwd_enter,
    bwd_in,
    bwd_enter,
    saved,
    fwd_routes,
    fwd_gates,
    bwd_routes,
    bwd_gates,
    gain,
    w_gate,
    w_up,
    w_down,
    fwd_out,
    bwd_out,
    in_f,
    enter_f,
    in_b,
    enter_b,
    in_s,
    routes_f,
    gates_f,
    routes_b,
    gates_b,
    gain_v,
    w_in,
    w_back,
    line_y,
    line_x,
    packed_x,
    packed_y,
    outgoing,
    partial_x,
    partial_y,
    landed_x,
    landed_y,
    middle,
    landed_two,
    hop_send,
    hop_land,
    pre_act,
    pick_x,
    pick_y,
    weight_of,
    load_sem,
    weight_send,
    weight_recv,
    gather_send,
    gather_recv,
    reduce_send,
    reduce_recv,
    hop_send_sem,
    hop_recv_sem,
):
    width = gain.shape[-1]
    half = width // 2
    unit = w_down.shape[0]
    rows = in_f.shape[0]
    tokens = SIDE * SIDE * rows
    section = lax.axis_index("section")
    place = lax.axis_index("expert")
    core = lax.rem(place, CORES)
    x = lax.rem(place // CORES, SIDE)
    y = place // (CORES * SIDE)

    def device(dy=0, dx=0, dc=0, dz=0):
        at_y, at_x = lax.rem(y + dy, SIDE), lax.rem(x + dx, SIDE)
        at_c = lax.rem(core + dc, CORES)
        return (lax.rem(section + dz, sections), (at_y * SIDE + at_x) * CORES + at_c)

    sibling = device(dc=1)
    following, preceding = device(dz=1), device(dz=sections - 1)
    along_y = [device(dy=k) for k in PEERS]
    along_x = [device(dx=k) for k in PEERS]

    barrier = pltpu.get_barrier_semaphore()
    greeted = [sibling, following, preceding] + along_y + along_x
    for other in greeted:
        pl.semaphore_signal(barrier, inc=1, device_id=other, device_id_type=MESH)

    small = [
        (fwd_in.at[0], in_f),
        (gain, gain_v),
        (saved.at[0], in_s),
        (bwd_in.at[0], in_b),
        (fwd_routes, routes_f),
        (fwd_gates, gates_f),
        (bwd_routes, routes_b),
        (bwd_gates, gates_b),
        (fwd_enter.at[0], enter_f),
        (bwd_enter.at[0], enter_b),
    ]
    own_weights = [
        (w_gate, w_in.at[:, pl.ds(0, unit)]),
        (w_up, w_in.at[:, pl.ds(2 * unit, unit)]),
        (w_down, w_back.at[pl.ds(0, unit), :]),
    ]
    sibling_weights = [
        (w_gate, w_in.at[:, pl.ds(unit, unit)]),
        (w_up, w_in.at[:, pl.ds(3 * unit, unit)]),
        (w_down, w_back.at[pl.ds(unit, unit), :]),
    ]
    loads = [
        pltpu.make_async_copy(source, target, load_sem.at[i])
        for i, (source, target) in enumerate(small + own_weights)
    ]
    for load in loads:
        load.start()
    for load in loads[: len(small)]:
        load.wait()

    gain_row = gain_v[...]
    first, second = pl.ds(0, half), pl.ds(half, half)

    def place_own(u, block):
        line_y[u, y] = block[:, :half]
        line_x[u, x] = block[:, half:]

    _, normed = normalize(in_f[...].astype(F32), gain_row)
    place_own(0, normed)
    scales = []
    for step in range(2):
        scale, normed = normalize(in_s[step].astype(F32), gain_row)
        scales.append(scale)
        place_own(1 + 3 * step, normed)
    place_own(2, in_b[...])

    pl.semaphore_wait(barrier, len(greeted))

    sent = []

    def start(copies):
        for copy in copies:
            copy.start()
        sent.extend(copies)
        return copies

    def arrive(copies):
        for copy in copies:
            copy.wait_recv()

    def remote(source, target, send, recv, index, other):
        return pltpu.make_async_remote_copy(
            src_ref=source,
            dst_ref=target,
            send_sem=send.at[index],
            recv_sem=recv.at[index],
            device_id=other,
            device_id_type=MESH,
        )

    blocks = SIDE * SIDE * CORES
    slots = SIDE * CAP
    whole = SIDE * slots

    def iota(shape, axis):
        return lax.broadcasted_iota(jnp.int32, shape, axis)

    def choose():
        experts = iota((SIDE, blocks * rows), 0)
        hits, lines = [], []
        for routes, gates in ((routes_f, gates_f), (routes_b, gates_b)):
            for step in range(2):
                chosen = [routes[step, k : k + 1] == experts for k in range(2)]
                hits.append(jnp.where(chosen[0] | chosen[1], 1.0, 0.0))
                own = [jnp.where(routes[step, k : k + 1] == y, gates[step, k : k + 1], 0.0) for k in range(2)]
                lines.append(own[0] + own[1])
        hit = jnp.concatenate(hits, axis=0)
        from_lane, to_lane = (iota((blocks * rows, blocks * rows), axis) for axis in (0, 1))
        earlier = (from_lane // rows == to_lane // rows) & (from_lane < to_lane)
        rank = jnp.dot(
            hit.astype(BF16), jnp.where(earlier, 1.0, 0.0).astype(BF16), preferred_element_type=F32
        )
        key = jnp.where(hit > 0.5, rank, 64.0)
        lane, spot = iota((blocks * rows, SIDE * rows), 0), iota((blocks * rows, SIDE * rows), 1)
        near = lax.rem(spot, rows)
        in_column = lane == (((spot // rows) * SIDE + x) * CORES + core) * rows + near
        in_row = lane == ((y * SIDE + spot // rows) * CORES + core) * rows + near
        keys = [
            jnp.dot(
                key.astype(BF16), jnp.where(at, 1.0, 0.0).astype(BF16), preferred_element_type=F32
            )
            for at in (in_column, in_row)
        ]
        slot, spot = iota((slots, SIDE * rows), 0), iota((slots, SIDE * rows), 1)
        aligned = spot // rows == slot // CAP
        number = lax.rem(slot, CAP).astype(F32)
        order = iota((whole, blocks * rows), 0)
        lanes = iota((whole, blocks * rows), 1)
        block = (lax.rem(order // CAP, SIDE) * SIDE + order // slots) * CORES + core
        mine = lanes // rows == block
        position = lax.rem(order, CAP).astype(F32)
        is_own = iota((SIDE, SIDE * rows), 0) == y
        is_own_wide = iota((SIDE, blocks * rows), 0) == y
        for r in range(4):
            part = slice(r * SIDE, (r + 1) * SIDE)
            own = jnp.sum(jnp.where(is_own, keys[0][part], 0.0), axis=0, keepdims=True)
            pick_x[r] = jnp.where(aligned & (own == number), 1.0, 0.0)
            for e in range(SIDE):
                here = keys[1][r * SIDE + e : r * SIDE + e + 1]
                pick_y[r, e * slots : (e + 1) * slots] = jnp.where(
                    aligned & (here == number), 1.0, 0.0
                )
            own = jnp.sum(jnp.where(is_own_wide, key[part], 0.0), axis=0, keepdims=True)
            weight_of[r] = jnp.sum(
                jnp.where(mine & (own == position), lines[r], 0.0), axis=-1, keepdims=True
            )

    order, other = iota((whole, whole), 0), iota((whole, whole), 1)
    turned = lax.rem(order // CAP, SIDE) * slots + (order // slots) * CAP + lax.rem(order, CAP)
    turn = jnp.where(turned == other, 1.0, 0.0).astype(BF16)

    def gather_one(u):
        out = []
        for k in range(len(PEERS)):
            spot = line_y.at[u, y]
            out.append(remote(spot, spot, gather_send, gather_recv, (u, 0, 0, k), along_y[k]))
            spot = line_x.at[u, x]
            out.append(remote(spot, spot, gather_send, gather_recv, (u, 0, 1, k), along_x[k]))
        return out

    tiles = slots // rows

    def gather_two(u, r):
        out = []
        block = line_y[u].reshape(SIDE * rows, half)
        packed = jnp.dot(pick_x[r].astype(BF16), block, preferred_element_type=F32)
        packed_x[u, x] = packed.astype(BF16).reshape(tiles, rows, half)
        for k in range(len(PEERS)):
            spot = packed_x.at[u, x]
            out.append(remote(spot, spot, gather_send, gather_recv, (u, 1, 0, k), along_x[k]))
        block = line_x[u].reshape(SIDE * rows, half)
        packed = jnp.dot(pick_y[r].astype(BF16), block, preferred_element_type=F32)
        outgoing[u] = packed.astype(BF16).reshape(SIDE, tiles, rows, half)
        for k, step in enumerate(PEERS):
            source, target = outgoing.at[u, lax.rem(y + step, SIDE)], packed_y.at[u, y]
            out.append(remote(source, target, gather_send, gather_recv, (u, 1, 1, k), along_y[k]))
        packed_y[u, y] = outgoing[u, y]
        return out

    def halves(u):
        by_row = jnp.dot(turn, packed_y[u].reshape(whole, half), preferred_element_type=F32)
        return packed_x[u].reshape(whole, half), by_row.astype(BF16)

    def reduce_one(u):
        out = []
        for k, step in enumerate(PEERS):
            source, target = partial_x.at[u, lax.rem(x + step, SIDE)], landed_x.at[u, k]
            out.append(remote(source, target, reduce_send, reduce_recv, (u, 0, 0, k), along_x[k]))
            source, target = partial_y.at[u, lax.rem(y + step, SIDE)], landed_y.at[u, y]
            out.append(remote(source, target, reduce_send, reduce_recv, (u, 0, 1, k), along_y[k]))
        landed_y[u, y] = partial_y[u, y]
        return out

    transposed = (((0,), (0,)), ((), ()))

    def reduce_two(u, r):
        total = partial_x[u, x].astype(F32)
        for k in range(len(PEERS)):
            total = total + landed_x[u, k].astype(F32)
        spread = lax.dot_general(
            pick_x[r].astype(BF16),
            total.astype(BF16).reshape(slots, half),
            transposed,
            preferred_element_type=F32,
        )
        middle[u, 0] = spread.astype(BF16).reshape(SIDE, rows, half)
        spread = lax.dot_general(
            pick_y[r].astype(BF16),
            landed_y[u].reshape(whole, half),
            transposed,
            preferred_element_type=F32,
        )
        middle[u, 1] = spread.astype(BF16).reshape(SIDE, rows, half)
        out = []
        for k, step in enumerate(PEERS):
            at_x, at_y = lax.rem(x + step, SIDE), lax.rem(y + step, SIDE)
            for part, (at, peers) in enumerate(((at_y, along_y), (at_x, along_x))):
                source, target = middle.at[u, part, at], landed_two.at[u, part, k]
                index = (u, 1, part, k)
                out.append(remote(source, target, reduce_send, reduce_recv, index, peers[k]))
        return out

    def reduce_end(u):
        sums = []
        for part, at in enumerate((y, x)):
            total = middle[u, part, at].astype(F32)
            for k in range(len(PEERS)):
                total = total + landed_two[u, part, k].astype(F32)
            sums.append(total)
        return jnp.concatenate(sums, axis=-1)

    def pre_activation(u):
        by_column, by_row = halves(u)
        both = jnp.dot(by_column, w_in[first, :], preferred_element_type=F32)
        return both + jnp.dot(by_row, w_in[second, :], preferred_element_type=F32)

    shape = (SIDE, tiles, rows, half)

    def turn_rows(array):
        return jnp.dot(turn, array, preferred_element_type=F32).astype(BF16)

    def forward(u, target, r):
        both = pre_activation(u)
        a, up = both[:, : 2 * unit], both[:, 2 * unit :]
        hidden = (a / (1.0 + jnp.exp(-a)) * up * weight_of[r]).astype(BF16)
        piece = jnp.dot(hidden, w_back[:, first], preferred_element_type=F32)
        partial_x[target] = piece.astype(BF16).reshape(shape)
        piece = jnp.dot(turn_rows(hidden), w_back[:, second], preferred_element_type=F32)
        partial_y[target] = piece.astype(BF16).reshape(shape)

    contract = (((1,), (1,)), ((), ()))

    def backward(u, target, both, r):
        a, up = both[:, : 2 * unit], both[:, 2 * unit :]
        by_column, by_row = halves(u)
        d_hidden = lax.dot_general(
            by_column, w_back[:, first], contract, preferred_element_type=F32
        ) + lax.dot_general(by_row, w_back[:, second], contract, preferred_element_type=F32)
        d_hidden = d_hidden * weight_of[r]
        sigma = 1.0 / (1.0 + jnp.exp(-a))
        d_gate = (d_hidden * up * sigma * (1.0 + a * (1.0 - sigma))).astype(BF16)
        d_up = (d_hidden * a * sigma).astype(BF16)
        grads = jnp.concatenate([d_gate, d_up], axis=-1)
        piece = lax.dot_general(grads, w_in[first, :], contract, preferred_element_type=F32)
        partial_x[target] = piece.astype(BF16).reshape(shape)
        piece = lax.dot_general(
            turn_rows(grads), w_in[second, :], contract, preferred_element_type=F32
        )
        partial_y[target] = piece.astype(BF16).reshape(shape)

    def forward_end(u, inputs):
        return (inputs.astype(F32) + reduce_end(u)).astype(BF16)

    def backward_end(u, step, upstream):
        inputs = in_s[step].astype(F32)
        scale = scales[step]
        product = reduce_end(u) * gain_row
        change = scale * product - inputs * scale**3 * jnp.mean(
            product * inputs, axis=-1, keepdims=True
        )
        return (upstream.astype(F32) + change).astype(BF16)

    def hop(i, block, other):
        hop_send[i] = block
        return start(
            [remote(hop_send.at[i], hop_land.at[i], hop_send_sem, hop_recv_sem, (i,), other)]
        )

    gather_f = start(gather_one(0))
    weights = [
        remote(source, target, weight_send, weight_recv, (i,), sibling)
        for i, (source, target) in enumerate(sibling_weights)
    ]
    start(weights)
    gather_s = start(gather_one(1))
    gather_g = start(gather_one(2))
    choose()
    arrive(gather_f)
    gather_f = start(gather_two(0, 0))
    arrive(gather_s)
    gather_s = start(gather_two(1, 2))
    arrive(gather_g)
    gather_g = start(gather_two(2, 2))
    for load in loads[len(small) :]:
        load.wait()
    arrive(weights)
    arrive(gather_f)
    forward(0, 0, 0)
    reduce_f = start(reduce_one(0))
    gather_n = start(gather_one(4))
    arrive(gather_s)
    both = pre_activation(1)
    arrive(gather_g)
    backward(2, 1, both, 2)
    reduce_b = start(reduce_one(1))
    arrive(reduce_f)
    reduce_f = start(reduce_two(0, 0))
    arrive(gather_n)
    gather_n = start(gather_two(4, 3))
    arrive(reduce_b)
    reduce_b = start(reduce_two(1, 2))
    arrive(reduce_f)
    outputs = forward_end(0, in_f[...])
    hop_f = hop(0, outputs, following)
    fwd_out[0, 0] = outputs
    arrive(reduce_b)
    outputs = backward_end(1, 0, in_b[...])
    hop_b = hop(1, outputs, preceding)
    bwd_out[0, 0] = outputs

    arrive(hop_f)
    moved_f = jnp.where(section == 0, enter_f[...].astype(F32), hop_land[0].astype(F32))
    _, normed = normalize(moved_f, gain_row)
    place_own(3, normed)
    gather_f = start(gather_one(3))
    arrive(hop_b)
    moved_b = jnp.where(
        section == sections - 1, enter_b[...].astype(F32), hop_land[1].astype(F32)
    ).astype(BF16)
    place_own(5, moved_b)
    gather_g = start(gather_one(5))
    arrive(gather_n)
    pre_act[...] = pre_activation(4)
    arrive(gather_f)
    gather_f = start(gather_two(3, 1))
    arrive(gather_g)
    gather_g = start(gather_two(5, 3))
    arrive(gather_f)
    forward(3, 2, 1)
    reduce_f = start(reduce_one(2))
    arrive(gather_g)
    backward(5, 3, pre_act[...], 3)
    reduce_b = start(reduce_one(3))
    arrive(reduce_f)
    reduce_f = start(reduce_two(2, 1))
    arrive(reduce_b)
    reduce_b = start(reduce_two(3, 3))
    arrive(reduce_f)
    fwd_out[0, 1] = forward_end(2, moved_f)
    arrive(reduce_b)
    bwd_out[0, 1] = backward_end(3, 1, moved_b)
    for copy in sent:
        copy.wait_send()


def per_device(
    fwd_in,
    fwd_enter,
    bwd_in,
    bwd_enter,
    saved,
    fwd_routes,
    fwd_gates,
    bwd_routes,
    bwd_gates,
    gain,
    w_gate,
    w_up,
    w_down,
):
    sections = lax.axis_size("section")
    steps, rows, width = saved.shape[1:]
    unit = w_gate.shape[-1]
    half = width // 2
    peers = len(PEERS)
    tiles = SIDE * CAP // rows
    turned = [
        jnp.transpose(array[0], (0, 2, 1)) for array in (fwd_routes, fwd_gates, bwd_routes, bwd_gates)
    ]
    in_hbm = pl.BlockSpec(memory_space=pltpu.HBM)
    in_vmem = pl.BlockSpec(memory_space=pltpu.VMEM)
    table = turned[0].shape
    dma = pltpu.SemaphoreType.DMA
    scratch = [
        pltpu.VMEM((rows, width), BF16),
        pltpu.VMEM((rows, width), BF16),
        pltpu.VMEM((rows, width), BF16),
        pltpu.VMEM((rows, width), BF16),
        pltpu.VMEM((steps, rows, width), BF16),
        pltpu.VMEM(table, jnp.int32),
        pltpu.VMEM(table, F32),
        pltpu.VMEM(table, jnp.int32),
        pltpu.VMEM(table, F32),
        pltpu.VMEM((1, width), F32),
        pltpu.VMEM((width, 4 * unit), BF16),
        pltpu.VMEM((2 * unit, width), BF16),
        pltpu.VMEM((6, SIDE, rows, half), BF16),
        pltpu.VMEM((6, SIDE, rows, half), BF16),
        pltpu.VMEM((6, SIDE, tiles, rows, half), BF16),
        pltpu.VMEM((6, SIDE, tiles, rows, half), BF16),
        pltpu.VMEM((6, SIDE, tiles, rows, half), BF16),
        pltpu.VMEM((4, SIDE, tiles, rows, half), BF16),
        pltpu.VMEM((4, SIDE, tiles, rows, half), BF16),
        pltpu.VMEM((4, peers, tiles, rows, half), BF16),
        pltpu.VMEM((4, SIDE, tiles, rows, half), BF16),
        pltpu.VMEM((4, 2, SIDE, rows, half), BF16),
        pltpu.VMEM((4, 2, peers, rows, half), BF16),
        pltpu.VMEM((2, rows, width), BF16),
        pltpu.VMEM((2, rows, width), BF16),
        pltpu.VMEM((SIDE * SIDE * CAP, 4 * unit), F32),
        pltpu.VMEM((4, SIDE * CAP, SIDE * rows), F32),
        pltpu.VMEM((4, SIDE * SIDE * CAP, SIDE * rows), F32),
        pltpu.VMEM((4, SIDE * SIDE * CAP, 1), F32),
        dma((13,)),
        dma((3,)),
        dma((3,)),
        dma((6, 2, 2, peers)),
        dma((6, 2, 2, peers)),
        dma((4, 2, 2, peers)),
        dma((4, 2, 2, peers)),
        dma((2,)),
        dma((2,)),
    ]
    out = jax.ShapeDtypeStruct((1, steps, rows, width), BF16)
    return pl.pallas_call(
        functools.partial(relay_kernel, sections),
        out_shape=(out, out),
        in_specs=[in_hbm] * 13,
        out_specs=(in_vmem, in_vmem),
        scratch_shapes=scratch,
        compiler_params=pltpu.CompilerParams(
            collective_id=0, has_side_effects=True, vmem_limit_bytes=60 * 2**20
        ),
        name="relay",
    )(
        fwd_in,
        fwd_enter,
        bwd_in,
        bwd_enter,
        saved,
        *turned,
        gain,
        w_gate[0],
        w_up[0],
        w_down[0],
    )


def solution(mesh):
    in_specs = (
        P("section", "expert", None),
        P(None, "expert", None),
        P("section", "expert", None),
        P(None, "expert", None),
        P("section", None, "expert", None),
        P("section", None, None, None),
        P("section", None, None, None),
        P("section", None, None, None),
        P("section", None, None, None),
        P("section", None),
        P("section", None, "expert"),
        P("section", None, "expert"),
        P("section", "expert", None),
    )
    out_specs = (P("section", None, "expert", None), P("section", None, "expert", None))
    return jax.shard_map(
        per_device, mesh=mesh, in_specs=in_specs, out_specs=out_specs, check_vma=False
    )
```

```python
import functools

import jax
import jax.numpy as jnp
from jax import lax
from jax.experimental import pallas as pl
from jax.experimental.pallas import tpu as pltpu
from jax.sharding import PartitionSpec as P

EPSILON = 1e-06
MESH = pl.DeviceIdType.MESH
SIDE = 4
CORES = 2
PEERS = (2, 1, 3)
CAP = 6
F32 = jnp.float32
BF16 = jnp.bfloat16


def normalize(inputs, gain):
    scale = lax.rsqrt(jnp.mean(inputs * inputs, axis=-1, keepdims=True) + EPSILON)
    return scale, (inputs * scale * gain).astype(BF16)


def relay_kernel(
    sections,
    fwd_in,
    fwd_enter,
    bwd_in,
    bwd_enter,
    saved,
    fwd_routes,
    fwd_gates,
    bwd_routes,
    bwd_gates,
    gain,
    w_gate,
    w_up,
    w_down,
    fwd_out,
    bwd_out,
    in_f,
    enter_f,
    in_b,
    enter_b,
    in_s,
    routes_f,
    gates_f,
    routes_b,
    gates_b,
    gain_v,
    w_in,
    w_back,
    line_y,
    line_x,
    packed_x,
    packed_y,
    outgoing,
    partial_x,
    partial_y,
    landed_x,
    landed_y,
    middle,
    landed_two,
    hop_send,
    hop_land,
    pre_act,
    pick_x,
    pick_y,
    weight_of,
    load_sem,
    weight_send,
    weight_recv,
    gather_send,
    gather_recv,
    reduce_send,
    reduce_recv,
    hop_send_sem,
    hop_recv_sem,
):
    width = gain.shape[-1]
    half = width // 2
    unit = w_down.shape[0]
    rows = in_f.shape[0]
    tokens = SIDE * SIDE * rows
    section = lax.axis_index("section")
    place = lax.axis_index("expert")
    core = lax.rem(place, CORES)
    x = lax.rem(place // CORES, SIDE)
    y = place // (CORES * SIDE)

    def device(dy=0, dx=0, dc=0, dz=0):
        at_y, at_x = lax.rem(y + dy, SIDE), lax.rem(x + dx, SIDE)
        at_c = lax.rem(core + dc, CORES)
        return (lax.rem(section + dz, sections), (at_y * SIDE + at_x) * CORES + at_c)

    sibling = device(dc=1)
    following, preceding = device(dz=1), device(dz=sections - 1)
    along_y = [device(dy=k) for k in PEERS]
    along_x = [device(dx=k) for k in PEERS]

    barrier = pltpu.get_barrier_semaphore()
    greeted = [sibling, following, preceding] + along_y + along_x
    for other in greeted:
        pl.semaphore_signal(barrier, inc=1, device_id=other, device_id_type=MESH)

    small = [
        (fwd_in.at[0], in_f),
        (gain, gain_v),
        (saved.at[0], in_s),
        (bwd_in.at[0], in_b),
        (fwd_routes, routes_f),
        (fwd_gates, gates_f),
        (bwd_routes, routes_b),
        (bwd_gates, gates_b),
        (fwd_enter.at[0], enter_f),
        (bwd_enter.at[0], enter_b),
    ]
    own_weights = [
        (w_gate, w_in.at[:, pl.ds(0, unit)]),
        (w_up, w_in.at[:, pl.ds(2 * unit, unit)]),
        (w_down, w_back.at[pl.ds(0, unit), :]),
    ]
    sibling_weights = [
        (w_gate, w_in.at[:, pl.ds(unit, unit)]),
        (w_up, w_in.at[:, pl.ds(3 * unit, unit)]),
        (w_down, w_back.at[pl.ds(unit, unit), :]),
    ]
    loads = [
        pltpu.make_async_copy(source, target, load_sem.at[i])
        for i, (source, target) in enumerate(small + own_weights)
    ]
    for load in loads:
        load.start()
    loads[1].wait()
    loads[2].wait()
    gain_row = gain_v[...]
    first, second = pl.ds(0, half), pl.ds(half, half)

    def place_own(u, block):
        line_y[u, y] = block[:, :half]
        line_x[u, x] = block[:, half:]

    scale, normed = normalize(in_s[0].astype(F32), gain_row)
    scales = [scale]
    place_own(1, normed)
    pl.semaphore_wait(barrier, len(greeted))

    sent = []

    def start(copies):
        for copy in copies:
            copy.start()
        sent.extend(copies)
        return copies

    def arrive(copies):
        for copy in copies:
            copy.wait_recv()

    def remote(source, target, send, recv, index, other):
        return pltpu.make_async_remote_copy(
            src_ref=source,
            dst_ref=target,
            send_sem=send.at[index],
            recv_sem=recv.at[index],
            device_id=other,
            device_id_type=MESH,
        )

    blocks = SIDE * SIDE * CORES
    slots = SIDE * CAP
    whole = SIDE * slots

    def iota(shape, axis):
        return lax.broadcasted_iota(jnp.int32, shape, axis)

    def choose():
        experts = iota((SIDE, blocks * rows), 0)
        hits, lines = [], []
        for routes, gates in ((routes_f, gates_f), (routes_b, gates_b)):
            for step in range(2):
                chosen = [routes[step, k : k + 1] == experts for k in range(2)]
                hits.append(jnp.where(chosen[0] | chosen[1], 1.0, 0.0))
                own = [jnp.where(routes[step, k : k + 1] == y, gates[step, k : k + 1], 0.0) for k in range(2)]
                lines.append(own[0] + own[1])
        hit = jnp.concatenate(hits, axis=0)
        from_lane, to_lane = (iota((blocks * rows, blocks * rows), axis) for axis in (0, 1))
        earlier = (from_lane // rows == to_lane // rows) & (from_lane < to_lane)
        rank = jnp.dot(
            hit.astype(BF16), jnp.where(earlier, 1.0, 0.0).astype(BF16), preferred_element_type=F32
        )
        key = jnp.where(hit > 0.5, rank, 64.0)
        lane, spot = iota((blocks * rows, SIDE * rows), 0), iota((blocks * rows, SIDE * rows), 1)
        near = lax.rem(spot, rows)
        in_column = lane == (((spot // rows) * SIDE + x) * CORES + core) * rows + near
        in_row = lane == ((y * SIDE + spot // rows) * CORES + core) * rows + near
        keys = [
            jnp.dot(
                key.astype(BF16), jnp.where(at, 1.0, 0.0).astype(BF16), preferred_element_type=F32
            )
            for at in (in_column, in_row)
        ]
        slot, spot = iota((slots, SIDE * rows), 0), iota((slots, SIDE * rows), 1)
        aligned = spot // rows == slot // CAP
        number = lax.rem(slot, CAP).astype(F32)
        order = iota((whole, blocks * rows), 0)
        lanes = iota((whole, blocks * rows), 1)
        block = (lax.rem(order // CAP, SIDE) * SIDE + order // slots) * CORES + core
        mine = lanes // rows == block
        position = lax.rem(order, CAP).astype(F32)
        is_own = iota((SIDE, SIDE * rows), 0) == y
        is_own_wide = iota((SIDE, blocks * rows), 0) == y
        for r in range(4):
            part = slice(r * SIDE, (r + 1) * SIDE)
            own = jnp.sum(jnp.where(is_own, keys[0][part], 0.0), axis=0, keepdims=True)
            pick_x[r] = jnp.where(aligned & (own == number), 1.0, 0.0)
            for e in range(SIDE):
                here = keys[1][r * SIDE + e : r * SIDE + e + 1]
                pick_y[r, e * slots : (e + 1) * slots] = jnp.where(
                    aligned & (here == number), 1.0, 0.0
                )
            own = jnp.sum(jnp.where(is_own_wide, key[part], 0.0), axis=0, keepdims=True)
            weight_of[r] = jnp.sum(
                jnp.where(mine & (own == position), lines[r], 0.0), axis=-1, keepdims=True
            )

    order, other = iota((whole, whole), 0), iota((whole, whole), 1)
    turned = lax.rem(order // CAP, SIDE) * slots + (order // slots) * CAP + lax.rem(order, CAP)
    turn = jnp.where(turned == other, 1.0, 0.0).astype(BF16)

    def gather_one(u):
        out = []
        for k in range(len(PEERS)):
            spot = line_y.at[u, y]
            out.append(remote(spot, spot, gather_send, gather_recv, (u, 0, 0, k), along_y[k]))
            spot = line_x.at[u, x]
            out.append(remote(spot, spot, gather_send, gather_recv, (u, 0, 1, k), along_x[k]))
        return out

    tiles = slots // rows

    def gather_two(u, r, ones):
        arrive(ones[0::2])
        block = line_y[u].reshape(SIDE * rows, half)
        packed = jnp.dot(pick_x[r].astype(BF16), block, preferred_element_type=F32)
        packed_x[u, x] = packed.astype(BF16).reshape(tiles, rows, half)
        spot = packed_x.at[u, x]
        across_x = start(
            [
                remote(spot, spot, gather_send, gather_recv, (u, 1, 0, k), along_x[k])
                for k in range(len(PEERS))
            ]
        )
        arrive(ones[1::2])
        block = line_x[u].reshape(SIDE * rows, half)
        packed = jnp.dot(pick_y[r].astype(BF16), block, preferred_element_type=F32)
        outgoing[u] = packed.astype(BF16).reshape(SIDE, tiles, rows, half)
        across_y = []
        for k, step in enumerate(PEERS):
            source, target = outgoing.at[u, lax.rem(y + step, SIDE)], packed_y.at[u, y]
            across_y.append(
                remote(source, target, gather_send, gather_recv, (u, 1, 1, k), along_y[k])
            )
        start(across_y)
        packed_y[u, y] = outgoing[u, y]
        return across_x, across_y

    def by_column(u):
        return packed_x[u].reshape(whole, half)

    def by_row(u):
        return turn_rows(packed_y[u].reshape(whole, half))

    def turn_rows(array):
        return jnp.dot(turn, array, preferred_element_type=F32).astype(BF16)

    def reduce_x(u):
        out = []
        for k, step in enumerate(PEERS):
            source, target = partial_x.at[u, lax.rem(x + step, SIDE)], landed_x.at[u, k]
            out.append(remote(source, target, reduce_send, reduce_recv, (u, 0, 0, k), along_x[k]))
        return start(out)

    def reduce_y(u):
        out = []
        for k, step in enumerate(PEERS):
            source, target = partial_y.at[u, lax.rem(y + step, SIDE)], landed_y.at[u, y]
            out.append(remote(source, target, reduce_send, reduce_recv, (u, 0, 1, k), along_y[k]))
        start(out)
        landed_y[u, y] = partial_y[u, y]
        return out

    transposed = (((0,), (0,)), ((), ()))

    def last_leg(u, part, at, peers):
        out = []
        for k, step in enumerate(PEERS):
            source, target = middle.at[u, part, lax.rem(at + step, SIDE)], landed_two.at[u, part, k]
            out.append(remote(source, target, reduce_send, reduce_recv, (u, 1, part, k), peers[k]))
        return start(out)

    def reduce_two(u, r, ones):
        arrive(ones[0])
        total = partial_x[u, x].astype(F32)
        for k in range(len(PEERS)):
            total = total + landed_x[u, k].astype(F32)
        spread = lax.dot_general(
            pick_x[r].astype(BF16),
            total.astype(BF16).reshape(slots, half),
            transposed,
            preferred_element_type=F32,
        )
        middle[u, 0] = spread.astype(BF16).reshape(SIDE, rows, half)
        across_y = last_leg(u, 0, y, along_y)
        arrive(ones[1])
        spread = lax.dot_general(
            pick_y[r].astype(BF16),
            landed_y[u].reshape(whole, half),
            transposed,
            preferred_element_type=F32,
        )
        middle[u, 1] = spread.astype(BF16).reshape(SIDE, rows, half)
        return across_y + last_leg(u, 1, x, along_x)

    def reduce_end(u):
        sums = []
        for part, at in enumerate((y, x)):
            total = middle[u, part, at].astype(F32)
            for k in range(len(PEERS)):
                total = total + landed_two[u, part, k].astype(F32)
            sums.append(total)
        return jnp.concatenate(sums, axis=-1)

    def pre_activation(u, twos):
        arrive(twos[0])
        both = jnp.dot(by_column(u), w_in[first, :], preferred_element_type=F32)
        arrive(twos[1])
        return both + jnp.dot(by_row(u), w_in[second, :], preferred_element_type=F32)

    shape = (SIDE, tiles, rows, half)

    def forward(target, r, both):
        a, up = both[:, : 2 * unit], both[:, 2 * unit :]
        hidden = (a / (1.0 + jnp.exp(-a)) * up * weight_of[r]).astype(BF16)
        piece = jnp.dot(hidden, w_back[:, first], preferred_element_type=F32)
        partial_x[target] = piece.astype(BF16).reshape(shape)
        across_x = reduce_x(target)
        piece = jnp.dot(turn_rows(hidden), w_back[:, second], preferred_element_type=F32)
        partial_y[target] = piece.astype(BF16).reshape(shape)
        return across_x, reduce_y(target)

    contract = (((1,), (1,)), ((), ()))

    def backward(u, target, both, r, twos):
        a, up = both[:, : 2 * unit], both[:, 2 * unit :]
        arrive(twos[0])
        d_hidden = lax.dot_general(
            by_column(u), w_back[:, first], contract, preferred_element_type=F32
        )
        arrive(twos[1])
        d_hidden = d_hidden + lax.dot_general(
            by_row(u), w_back[:, second], contract, preferred_element_type=F32
        )
        d_hidden = d_hidden * weight_of[r]
        sigma = 1.0 / (1.0 + jnp.exp(-a))
        d_gate = (d_hidden * up * sigma * (1.0 + a * (1.0 - sigma))).astype(BF16)
        d_up = (d_hidden * a * sigma).astype(BF16)
        grads = jnp.concatenate([d_gate, d_up], axis=-1)
        piece = lax.dot_general(grads, w_in[first, :], contract, preferred_element_type=F32)
        partial_x[target] = piece.astype(BF16).reshape(shape)
        across_x = reduce_x(target)
        piece = lax.dot_general(
            turn_rows(grads), w_in[second, :], contract, preferred_element_type=F32
        )
        partial_y[target] = piece.astype(BF16).reshape(shape)
        return across_x, reduce_y(target)

    def forward_end(u, inputs):
        return (inputs.astype(F32) + reduce_end(u)).astype(BF16)

    def backward_end(u, step, upstream):
        inputs = in_s[step].astype(F32)
        scale = scales[step]
        product = reduce_end(u) * gain_row
        change = scale * product - inputs * scale**3 * jnp.mean(
            product * inputs, axis=-1, keepdims=True
        )
        return (upstream.astype(F32) + change).astype(BF16)

    def hop(i, block, other):
        hop_send[i] = block
        return start(
            [remote(hop_send.at[i], hop_land.at[i], hop_send_sem, hop_recv_sem, (i,), other)]
        )

    for load in [loads[0]] + loads[3 : len(small)]:
        load.wait()
    place_own(2, in_b[...])
    gather_s = start(gather_one(1))
    gather_g = start(gather_one(2))
    weights = [
        remote(source, target, weight_send, weight_recv, (i,), sibling)
        for i, (source, target) in enumerate(sibling_weights)
    ]
    start(weights)
    _, normed = normalize(in_f[...].astype(F32), gain_row)
    place_own(0, normed)
    gather_f = start(gather_one(0))
    scale, normed = normalize(in_s[1].astype(F32), gain_row)
    scales.append(scale)
    place_own(4, normed)
    choose()
    gather_s = gather_two(1, 2, gather_s)
    gather_g = gather_two(2, 2, gather_g)
    gather_f = gather_two(0, 0, gather_f)
    for load in loads[len(small) :]:
        load.wait()
    arrive(weights)
    both = pre_activation(1, gather_s)
    reduce_b = backward(2, 1, both, 2, gather_g)
    both = pre_activation(0, gather_f)
    reduce_f = forward(0, 0, both)
    gather_n = start(gather_one(4))
    reduce_b = reduce_two(1, 2, reduce_b)
    reduce_f = reduce_two(0, 0, reduce_f)
    arrive(reduce_b)
    outputs = backward_end(1, 0, in_b[...])
    hop_b = hop(1, outputs, preceding)
    bwd_out[0, 0] = outputs
    gather_n = gather_two(4, 3, gather_n)
    arrive(reduce_f)
    outputs = forward_end(0, in_f[...])
    hop_f = hop(0, outputs, following)
    fwd_out[0, 0] = outputs

    arrive(hop_b)
    moved_b = jnp.where(
        section == sections - 1, enter_b[...].astype(F32), hop_land[1].astype(F32)
    ).astype(BF16)
    place_own(5, moved_b)
    gather_g = start(gather_one(5))
    arrive(hop_f)
    moved_f = jnp.where(section == 0, enter_f[...].astype(F32), hop_land[0].astype(F32))
    _, normed = normalize(moved_f, gain_row)
    place_own(3, normed)
    gather_f = start(gather_one(3))
    pre_act[...] = pre_activation(4, gather_n)
    gather_g = gather_two(5, 3, gather_g)
    gather_f = gather_two(3, 1, gather_f)
    reduce_b = backward(5, 3, pre_act[...], 3, gather_g)
    both = pre_activation(3, gather_f)
    reduce_f = forward(2, 1, both)
    reduce_b = reduce_two(3, 3, reduce_b)
    reduce_f = reduce_two(2, 1, reduce_f)
    arrive(reduce_b)
    bwd_out[0, 1] = backward_end(3, 1, moved_b)
    arrive(reduce_f)
    fwd_out[0, 1] = forward_end(2, moved_f)
    for copy in sent:
        copy.wait_send()


def per_device(
    fwd_in,
    fwd_enter,
    bwd_in,
    bwd_enter,
    saved,
    fwd_routes,
    fwd_gates,
    bwd_routes,
    bwd_gates,
    gain,
    w_gate,
    w_up,
    w_down,
):
    sections = lax.axis_size("section")
    steps, rows, width = saved.shape[1:]
    unit = w_gate.shape[-1]
    half = width // 2
    peers = len(PEERS)
    tiles = SIDE * CAP // rows
    turned = [
        jnp.transpose(array[0], (0, 2, 1)) for array in (fwd_routes, fwd_gates, bwd_routes, bwd_gates)
    ]
    in_hbm = pl.BlockSpec(memory_space=pltpu.HBM)
    in_vmem = pl.BlockSpec(memory_space=pltpu.VMEM)
    table = turned[0].shape
    dma = pltpu.SemaphoreType.DMA
    scratch = [
        pltpu.VMEM((rows, width), BF16),
        pltpu.VMEM((rows, width), BF16),
        pltpu.VMEM((rows, width), BF16),
        pltpu.VMEM((rows, width), BF16),
        pltpu.VMEM((steps, rows, width), BF16),
        pltpu.VMEM(table, jnp.int32),
        pltpu.VMEM(table, F32),
        pltpu.VMEM(table, jnp.int32),
        pltpu.VMEM(table, F32),
        pltpu.VMEM((1, width), F32),
        pltpu.VMEM((width, 4 * unit), BF16),
        pltpu.VMEM((2 * unit, width), BF16),
        pltpu.VMEM((6, SIDE, rows, half), BF16),
        pltpu.VMEM((6, SIDE, rows, half), BF16),
        pltpu.VMEM((6, SIDE, tiles, rows, half), BF16),
        pltpu.VMEM((6, SIDE, tiles, rows, half), BF16),
        pltpu.VMEM((6, SIDE, tiles, rows, half), BF16),
        pltpu.VMEM((4, SIDE, tiles, rows, half), BF16),
        pltpu.VMEM((4, SIDE, tiles, rows, half), BF16),
        pltpu.VMEM((4, peers, tiles, rows, half), BF16),
        pltpu.VMEM((4, SIDE, tiles, rows, half), BF16),
        pltpu.VMEM((4, 2, SIDE, rows, half), BF16),
        pltpu.VMEM((4, 2, peers, rows, half), BF16),
        pltpu.VMEM((2, rows, width), BF16),
        pltpu.VMEM((2, rows, width), BF16),
        pltpu.VMEM((SIDE * SIDE * CAP, 4 * unit), F32),
        pltpu.VMEM((4, SIDE * CAP, SIDE * rows), F32),
        pltpu.VMEM((4, SIDE * SIDE * CAP, SIDE * rows), F32),
        pltpu.VMEM((4, SIDE * SIDE * CAP, 1), F32),
        dma((13,)),
        dma((3,)),
        dma((3,)),
        dma((6, 2, 2, peers)),
        dma((6, 2, 2, peers)),
        dma((4, 2, 2, peers)),
        dma((4, 2, 2, peers)),
        dma((2,)),
        dma((2,)),
    ]
    out = jax.ShapeDtypeStruct((1, steps, rows, width), BF16)
    results = pl.pallas_call(
        functools.partial(relay_kernel, sections),
        out_shape=(out, out),
        in_specs=[in_hbm] * 13,
        out_specs=(in_vmem, in_vmem),
        scratch_shapes=scratch,
        compiler_params=pltpu.CompilerParams(
            collective_id=0, has_side_effects=True, vmem_limit_bytes=60 * 2**20
        ),
        name="relay",
    )(
        fwd_in,
        fwd_enter,
        bwd_in,
        bwd_enter,
        saved,
        *turned,
        gain,
        w_gate[0],
        w_up[0],
        w_down[0],
    )
    return pl.pallas_call(
        store_kernel,
        out_shape=(out, out),
        in_specs=[pl.BlockSpec(memory_space=pltpu.VMEM)] * 2,
        out_specs=(pl.BlockSpec(memory_space=pl.ANY),) * 2,
        scratch_shapes=[dma((2,))],
        name="store",
    )(*results)


def store_kernel(fwd, bwd, fwd_to, bwd_to, sems):
    copies = [
        pltpu.make_async_copy(source, target, sems.at[i])
        for i, (source, target) in enumerate(((fwd, fwd_to), (bwd, bwd_to)))
    ]
    for copy in copies:
        copy.start()
    for copy in copies:
        copy.wait()


def solution(mesh):
    in_specs = (
        P("section", "expert", None),
        P(None, "expert", None),
        P("section", "expert", None),
        P(None, "expert", None),
        P("section", None, "expert", None),
        P("section", None, None, None),
        P("section", None, None, None),
        P("section", None, None, None),
        P("section", None, None, None),
        P("section", None),
        P("section", None, "expert"),
        P("section", None, "expert"),
        P("section", "expert", None),
    )
    out_specs = (P("section", None, "expert", None), P("section", None, "expert", None))
    return jax.shard_map(
        per_device, mesh=mesh, in_specs=in_specs, out_specs=out_specs, check_vma=False
    )
```

```python
import functools

import jax
import jax.numpy as jnp
from jax import lax
from jax.experimental import pallas as pl
from jax.experimental.pallas import tpu as pltpu
from jax.sharding import PartitionSpec as P

EPSILON = 1e-06
MESH = pl.DeviceIdType.MESH
SIDE = 4
CORES = 2
PEERS = (2, 1, 3)
CAP = 6
F32 = jnp.float32
BF16 = jnp.bfloat16


def normalize(inputs, gain):
    scale = lax.rsqrt(jnp.mean(inputs * inputs, axis=-1, keepdims=True) + EPSILON)
    return scale, (inputs * scale * gain).astype(BF16)


def relay_kernel(
    sections,
    fwd_in,
    fwd_enter,
    bwd_in,
    bwd_enter,
    saved,
    fwd_routes,
    fwd_gates,
    bwd_routes,
    bwd_gates,
    gain,
    w_gate,
    w_up,
    w_down,
    fwd_out,
    bwd_out,
    in_f,
    enter_f,
    in_b,
    enter_b,
    in_s,
    routes_f,
    gates_f,
    routes_b,
    gates_b,
    gain_v,
    w_in,
    w_back,
    w_in_turned,
    line_y,
    line_x,
    packed_x,
    packed_y,
    outgoing,
    partial_x,
    partial_y,
    landed_x,
    landed_y,
    middle,
    landed_two,
    hop_send,
    hop_land,
    pre_act,
    pick_x,
    pick_y,
    weight_of,
    load_sem,
    weight_send,
    weight_recv,
    gather_send,
    gather_recv,
    reduce_send,
    reduce_recv,
    hop_send_sem,
    hop_recv_sem,
):
    width = gain.shape[-1]
    half = width // 2
    unit = w_down.shape[0]
    rows = in_f.shape[0]
    tokens = SIDE * SIDE * rows
    section = lax.axis_index("section")
    place = lax.axis_index("expert")
    core = lax.rem(place, CORES)
    x = lax.rem(place // CORES, SIDE)
    y = place // (CORES * SIDE)

    def device(dy=0, dx=0, dc=0, dz=0):
        at_y, at_x = lax.rem(y + dy, SIDE), lax.rem(x + dx, SIDE)
        at_c = lax.rem(core + dc, CORES)
        return (lax.rem(section + dz, sections), (at_y * SIDE + at_x) * CORES + at_c)

    sibling = device(dc=1)
    following, preceding = device(dz=1), device(dz=sections - 1)
    along_y = [device(dy=k) for k in PEERS]
    along_x = [device(dx=k) for k in PEERS]

    barrier = pltpu.get_barrier_semaphore()
    greeted = [sibling, following, preceding] + along_y + along_x
    for other in greeted:
        pl.semaphore_signal(barrier, inc=1, device_id=other, device_id_type=MESH)

    small = [
        (fwd_in.at[0], in_f),
        (gain, gain_v),
        (saved.at[0], in_s),
        (bwd_in.at[0], in_b),
        (fwd_routes, routes_f),
        (fwd_gates, gates_f),
        (bwd_routes, routes_b),
        (bwd_gates, gates_b),
        (fwd_enter.at[0], enter_f),
        (bwd_enter.at[0], enter_b),
    ]
    own_weights = [
        (w_gate, w_in.at[:, pl.ds(0, unit)]),
        (w_up, w_in.at[:, pl.ds(2 * unit, unit)]),
        (w_down, w_back.at[pl.ds(0, unit), :]),
    ]
    sibling_weights = [
        (w_gate, w_in.at[:, pl.ds(unit, unit)]),
        (w_up, w_in.at[:, pl.ds(3 * unit, unit)]),
        (w_down, w_back.at[pl.ds(unit, unit), :]),
    ]
    loads = [
        pltpu.make_async_copy(source, target, load_sem.at[i])
        for i, (source, target) in enumerate(small + own_weights)
    ]
    for load in loads:
        load.start()
    loads[1].wait()
    loads[2].wait()
    gain_row = gain_v[...]
    quarter = half // 2
    first, second = pl.ds(0, half), pl.ds(half, half)
    parts = [pl.ds(c * quarter, quarter) for c in range(2)]
    second_parts = [pl.ds(half + c * quarter, quarter) for c in range(2)]

    def place_own(u, block):
        line_y[u, y] = block[:, :half]
        line_x[u, x] = block[:, half:]

    scale, normed = normalize(in_s[0].astype(F32), gain_row)
    scales = [scale]
    place_own(1, normed)
    pl.semaphore_wait(barrier, len(greeted))

    sent = []

    def start(copies):
        for copy in copies:
            copy.start()
        sent.extend(copies)
        return copies

    def arrive(copies):
        for copy in copies:
            copy.wait_recv()

    def remote(source, target, send, recv, index, other):
        return pltpu.make_async_remote_copy(
            src_ref=source,
            dst_ref=target,
            send_sem=send.at[index],
            recv_sem=recv.at[index],
            device_id=other,
            device_id_type=MESH,
        )

    blocks = SIDE * SIDE * CORES
    slots = SIDE * CAP
    whole = SIDE * slots

    def iota(shape, axis):
        return lax.broadcasted_iota(jnp.int32, shape, axis)

    def choose():
        experts = iota((SIDE, blocks * rows), 0)
        hits, lines = [], []
        for routes, gates in ((routes_f, gates_f), (routes_b, gates_b)):
            for step in range(2):
                chosen = [routes[step, k : k + 1] == experts for k in range(2)]
                hits.append(jnp.where(chosen[0] | chosen[1], 1.0, 0.0))
                own = [jnp.where(routes[step, k : k + 1] == y, gates[step, k : k + 1], 0.0) for k in range(2)]
                lines.append(own[0] + own[1])
        hit = jnp.concatenate(hits, axis=0)
        from_lane, to_lane = (iota((blocks * rows, blocks * rows), axis) for axis in (0, 1))
        earlier = (from_lane // rows == to_lane // rows) & (from_lane < to_lane)
        rank = jnp.dot(
            hit.astype(BF16), jnp.where(earlier, 1.0, 0.0).astype(BF16), preferred_element_type=F32
        )
        key = jnp.where(hit > 0.5, rank, 64.0)
        lane, spot = iota((blocks * rows, SIDE * rows), 0), iota((blocks * rows, SIDE * rows), 1)
        near = lax.rem(spot, rows)
        in_column = lane == (((spot // rows) * SIDE + x) * CORES + core) * rows + near
        in_row = lane == ((y * SIDE + spot // rows) * CORES + core) * rows + near
        keys = [
            jnp.dot(
                key.astype(BF16), jnp.where(at, 1.0, 0.0).astype(BF16), preferred_element_type=F32
            )
            for at in (in_column, in_row)
        ]
        slot, spot = iota((slots, SIDE * rows), 0), iota((slots, SIDE * rows), 1)
        aligned = spot // rows == slot // CAP
        number = lax.rem(slot, CAP).astype(F32)
        order = iota((whole, blocks * rows), 0)
        lanes = iota((whole, blocks * rows), 1)
        block = (lax.rem(order // CAP, SIDE) * SIDE + order // slots) * CORES + core
        mine = lanes // rows == block
        position = lax.rem(order, CAP).astype(F32)
        is_own = iota((SIDE, SIDE * rows), 0) == y
        is_own_wide = iota((SIDE, blocks * rows), 0) == y
        for r in range(4):
            part = slice(r * SIDE, (r + 1) * SIDE)
            own = jnp.sum(jnp.where(is_own, keys[0][part], 0.0), axis=0, keepdims=True)
            pick_x[r] = jnp.where(aligned & (own == number), 1.0, 0.0)
            for e in range(SIDE):
                here = keys[1][r * SIDE + e : r * SIDE + e + 1]
                pick_y[r, e * slots : (e + 1) * slots] = jnp.where(
                    aligned & (here == number), 1.0, 0.0
                )
            own = jnp.sum(jnp.where(is_own_wide, key[part], 0.0), axis=0, keepdims=True)
            weight_of[r] = jnp.sum(
                jnp.where(mine & (own == position), lines[r], 0.0), axis=-1, keepdims=True
            )

    order, other = iota((whole, whole), 0), iota((whole, whole), 1)
    turned = lax.rem(order // CAP, SIDE) * slots + (order // slots) * CAP + lax.rem(order, CAP)
    turn = jnp.where(turned == other, 1.0, 0.0).astype(BF16)

    def gather_one(u):
        out = []
        for k in range(len(PEERS)):
            spot = line_y.at[u, y]
            out.append(remote(spot, spot, gather_send, gather_recv, (u, 0, 0, k), along_y[k]))
            spot = line_x.at[u, x]
            out.append(remote(spot, spot, gather_send, gather_recv, (u, 0, 1, k), along_x[k]))
        return out

    tiles = slots // rows

    def gather_two(u, r, ones):
        arrive(ones[0::2])
        block = line_y[u].reshape(SIDE * rows, half)
        packed = jnp.dot(pick_x[r].astype(BF16), block, preferred_element_type=F32)
        packed_x[u, x] = packed.astype(BF16).reshape(tiles, rows, half)
        spot = packed_x.at[u, x]
        across_x = start(
            [
                remote(spot, spot, gather_send, gather_recv, (u, 1, 0, k), along_x[k])
                for k in range(len(PEERS))
            ]
        )
        arrive(ones[1::2])
        block = line_x[u].reshape(SIDE * rows, half)
        packed = jnp.dot(pick_y[r].astype(BF16), block, preferred_element_type=F32)
        outgoing[u] = packed.astype(BF16).reshape(SIDE, tiles, rows, half)
        across_y = []
        for k, step in enumerate(PEERS):
            source, target = outgoing.at[u, lax.rem(y + step, SIDE)], packed_y.at[u, y]
            across_y.append(
                remote(source, target, gather_send, gather_recv, (u, 1, 1, k), along_y[k])
            )
        start(across_y)
        packed_y[u, y] = outgoing[u, y]
        return across_x, across_y

    def by_column(u):
        return packed_x[u].reshape(whole, half)

    def by_row(u):
        return turn_rows(packed_y[u].reshape(whole, half))

    def turn_rows(array):
        return jnp.dot(turn, array, preferred_element_type=F32).astype(BF16)

    def reduce_x(u, c):
        out = []
        for k, step in enumerate(PEERS):
            source = partial_x.at[u, lax.rem(x + step, SIDE), :, :, parts[c]]
            target = landed_x.at[u, k, :, :, parts[c]]
            index = (u, 0, 0, c, k)
            out.append(remote(source, target, reduce_send, reduce_recv, index, along_x[k]))
        return start(out)

    def reduce_y(u, c):
        out = []
        for k, step in enumerate(PEERS):
            source = partial_y.at[u, lax.rem(y + step, SIDE), :, :, parts[c]]
            target = landed_y.at[u, y, :, :, parts[c]]
            index = (u, 0, 1, c, k)
            out.append(remote(source, target, reduce_send, reduce_recv, index, along_y[k]))
        start(out)
        landed_y[u, y, :, :, parts[c]] = partial_y[u, y, :, :, parts[c]]
        return out

    transposed = (((0,), (0,)), ((), ()))

    def last_leg(u, part, c, at, peers):
        out = []
        for k, step in enumerate(PEERS):
            source = middle.at[u, part, lax.rem(at + step, SIDE), :, parts[c]]
            target = landed_two.at[u, part, k, :, parts[c]]
            index = (u, 1, part, c, k)
            out.append(remote(source, target, reduce_send, reduce_recv, index, peers[k]))
        return start(out)

    def reduce_two(u, r, ones):
        out = []
        for c in range(2):
            arrive(ones[c][0])
            total = partial_x[u, x, :, :, parts[c]].astype(F32)
            for k in range(len(PEERS)):
                total = total + landed_x[u, k, :, :, parts[c]].astype(F32)
            spread = lax.dot_general(
                pick_x[r].astype(BF16),
                total.astype(BF16).reshape(slots, quarter),
                transposed,
                preferred_element_type=F32,
            )
            middle[u, 0, :, :, parts[c]] = spread.astype(BF16).reshape(SIDE, rows, quarter)
            out += last_leg(u, 0, c, y, along_y)
            arrive(ones[c][1])
            spread = lax.dot_general(
                pick_y[r].astype(BF16),
                landed_y[u, :, :, :, parts[c]].reshape(whole, quarter),
                transposed,
                preferred_element_type=F32,
            )
            middle[u, 1, :, :, parts[c]] = spread.astype(BF16).reshape(SIDE, rows, quarter)
            out += last_leg(u, 1, c, x, along_x)
        return out

    def reduce_end(u):
        sums = []
        for part, at in enumerate((y, x)):
            total = middle[u, part, at].astype(F32)
            for k in range(len(PEERS)):
                total = total + landed_two[u, part, k].astype(F32)
            sums.append(total)
        return jnp.concatenate(sums, axis=-1)

    def pre_activation(u, twos):
        arrive(twos[0])
        both = jnp.dot(by_column(u), w_in[first, :], preferred_element_type=F32)
        arrive(twos[1])
        return both + jnp.dot(by_row(u), w_in[second, :], preferred_element_type=F32)

    shape = (SIDE, tiles, rows, quarter)

    def forward(target, r, both):
        a, up = both[:, : 2 * unit], both[:, 2 * unit :]
        hidden = (a / (1.0 + jnp.exp(-a)) * up * weight_of[r]).astype(BF16)
        hidden_turned = turn_rows(hidden)
        out = []
        for c in range(2):
            piece = jnp.dot(hidden, w_back[:, parts[c]], preferred_element_type=F32)
            partial_x[target, :, :, :, parts[c]] = piece.astype(BF16).reshape(shape)
            across_x = reduce_x(target, c)
            piece = jnp.dot(hidden_turned, w_back[:, second_parts[c]], preferred_element_type=F32)
            partial_y[target, :, :, :, parts[c]] = piece.astype(BF16).reshape(shape)
            out.append((across_x, reduce_y(target, c)))
        return out

    contract = (((1,), (1,)), ((), ()))

    def backward(u, target, both, r, twos):
        a, up = both[:, : 2 * unit], both[:, 2 * unit :]
        arrive(twos[0])
        d_hidden = lax.dot_general(
            by_column(u), w_back[:, first], contract, preferred_element_type=F32
        )
        arrive(twos[1])
        d_hidden = d_hidden + lax.dot_general(
            by_row(u), w_back[:, second], contract, preferred_element_type=F32
        )
        d_hidden = d_hidden * weight_of[r]
        sigma = 1.0 / (1.0 + jnp.exp(-a))
        d_gate = (d_hidden * up * sigma * (1.0 + a * (1.0 - sigma))).astype(BF16)
        d_up = (d_hidden * a * sigma).astype(BF16)
        grads = jnp.concatenate([d_gate, d_up], axis=-1)
        grads_turned = turn_rows(grads)
        out = []
        for c in range(2):
            piece = jnp.dot(grads, w_in_turned[:, parts[c]], preferred_element_type=F32)
            partial_x[target, :, :, :, parts[c]] = piece.astype(BF16).reshape(shape)
            across_x = reduce_x(target, c)
            piece = jnp.dot(grads_turned, w_in_turned[:, second_parts[c]], preferred_element_type=F32)
            partial_y[target, :, :, :, parts[c]] = piece.astype(BF16).reshape(shape)
            out.append((across_x, reduce_y(target, c)))
        return out

    def turn_weights():
        span = 2 * unit
        eye = jnp.where(iota((span, span), 0) == iota((span, span), 1), 1.0, 0.0).astype(BF16)
        for i in range(2):
            for rows_of in (first, second):
                turned_part = lax.dot_general(
                    eye,
                    w_in[rows_of, pl.ds(i * span, span)],
                    contract,
                    preferred_element_type=F32,
                )
                w_in_turned[pl.ds(i * span, span), rows_of] = turned_part.astype(BF16)

    def forward_end(u, inputs):
        return (inputs.astype(F32) + reduce_end(u)).astype(BF16)

    def backward_end(u, step, upstream):
        inputs = in_s[step].astype(F32)
        scale = scales[step]
        product = reduce_end(u) * gain_row
        change = scale * product - inputs * scale**3 * jnp.mean(
            product * inputs, axis=-1, keepdims=True
        )
        return (upstream.astype(F32) + change).astype(BF16)

    def hop(i, block, other):
        hop_send[i] = block
        return start(
            [remote(hop_send.at[i], hop_land.at[i], hop_send_sem, hop_recv_sem, (i,), other)]
        )

    for load in [loads[0]] + loads[3 : len(small)]:
        load.wait()
    place_own(2, in_b[...])
    gather_s = start(gather_one(1))
    gather_g = start(gather_one(2))
    weights = [
        remote(source, target, weight_send, weight_recv, (i,), sibling)
        for i, (source, target) in enumerate(sibling_weights)
    ]
    start(weights)
    _, normed = normalize(in_f[...].astype(F32), gain_row)
    place_own(0, normed)
    gather_f = start(gather_one(0))
    scale, normed = normalize(in_s[1].astype(F32), gain_row)
    scales.append(scale)
    place_own(4, normed)
    choose()
    gather_s = gather_two(1, 2, gather_s)
    gather_g = gather_two(2, 2, gather_g)
    gather_f = gather_two(0, 0, gather_f)
    gather_n = start(gather_one(4))
    for load in loads[len(small) :]:
        load.wait()
    arrive(weights)
    turn_weights()
    both = pre_activation(1, gather_s)
    reduce_b = backward(2, 1, both, 2, gather_g)
    both = pre_activation(0, gather_f)
    reduce_f = forward(0, 0, both)
    reduce_b = reduce_two(1, 2, reduce_b)
    reduce_f = reduce_two(0, 0, reduce_f)
    gather_n = gather_two(4, 3, gather_n)
    arrive(reduce_b)
    outputs = backward_end(1, 0, in_b[...])
    hop_b = hop(1, outputs, preceding)
    arrive(reduce_f)
    outputs = forward_end(0, in_f[...])
    hop_f = hop(0, outputs, following)
    bwd_out[0, 0] = hop_send[1]
    fwd_out[0, 0] = hop_send[0]

    arrive(hop_b)
    moved_b = jnp.where(
        section == sections - 1, enter_b[...].astype(F32), hop_land[1].astype(F32)
    ).astype(BF16)
    place_own(5, moved_b)
    gather_g = start(gather_one(5))
    arrive(hop_f)
    moved_f = jnp.where(section == 0, enter_f[...].astype(F32), hop_land[0].astype(F32))
    _, normed = normalize(moved_f, gain_row)
    place_own(3, normed)
    gather_f = start(gather_one(3))
    gather_g = gather_two(5, 3, gather_g)
    gather_f = gather_two(3, 1, gather_f)
    pre_act[...] = pre_activation(4, gather_n)
    reduce_b = backward(5, 3, pre_act[...], 3, gather_g)
    both = pre_activation(3, gather_f)
    reduce_f = forward(2, 1, both)
    reduce_b = reduce_two(3, 3, reduce_b)
    reduce_f = reduce_two(2, 1, reduce_f)
    arrive(reduce_b)
    bwd_out[0, 1] = backward_end(3, 1, moved_b)
    arrive(reduce_f)
    fwd_out[0, 1] = forward_end(2, moved_f)
    for copy in sent:
        copy.wait_send()


def per_device(
    fwd_in,
    fwd_enter,
    bwd_in,
    bwd_enter,
    saved,
    fwd_routes,
    fwd_gates,
    bwd_routes,
    bwd_gates,
    gain,
    w_gate,
    w_up,
    w_down,
):
    sections = lax.axis_size("section")
    steps, rows, width = saved.shape[1:]
    unit = w_gate.shape[-1]
    half = width // 2
    peers = len(PEERS)
    tiles = SIDE * CAP // rows
    turned = [
        jnp.transpose(array[0], (0, 2, 1)) for array in (fwd_routes, fwd_gates, bwd_routes, bwd_gates)
    ]
    in_hbm = pl.BlockSpec(memory_space=pltpu.HBM)
    in_vmem = pl.BlockSpec(memory_space=pltpu.VMEM)
    table = turned[0].shape
    dma = pltpu.SemaphoreType.DMA
    scratch = [
        pltpu.VMEM((rows, width), BF16),
        pltpu.VMEM((rows, width), BF16),
        pltpu.VMEM((rows, width), BF16),
        pltpu.VMEM((rows, width), BF16),
        pltpu.VMEM((steps, rows, width), BF16),
        pltpu.VMEM(table, jnp.int32),
        pltpu.VMEM(table, F32),
        pltpu.VMEM(table, jnp.int32),
        pltpu.VMEM(table, F32),
        pltpu.VMEM((1, width), F32),
        pltpu.VMEM((width, 4 * unit), BF16),
        pltpu.VMEM((2 * unit, width), BF16),
        pltpu.VMEM((4 * unit, width), BF16),
        pltpu.VMEM((6, SIDE, rows, half), BF16),
        pltpu.VMEM((6, SIDE, rows, half), BF16),
        pltpu.VMEM((6, SIDE, tiles, rows, half), BF16),
        pltpu.VMEM((6, SIDE, tiles, rows, half), BF16),
        pltpu.VMEM((6, SIDE, tiles, rows, half), BF16),
        pltpu.VMEM((4, SIDE, tiles, rows, half), BF16),
        pltpu.VMEM((4, SIDE, tiles, rows, half), BF16),
        pltpu.VMEM((4, peers, tiles, rows, half), BF16),
        pltpu.VMEM((4, SIDE, tiles, rows, half), BF16),
        pltpu.VMEM((4, 2, SIDE, rows, half), BF16),
        pltpu.VMEM((4, 2, peers, rows, half), BF16),
        pltpu.VMEM((2, rows, width), BF16),
        pltpu.VMEM((2, rows, width), BF16),
        pltpu.VMEM((SIDE * SIDE * CAP, 4 * unit), F32),
        pltpu.VMEM((4, SIDE * CAP, SIDE * rows), F32),
        pltpu.VMEM((4, SIDE * SIDE * CAP, SIDE * rows), F32),
        pltpu.VMEM((4, SIDE * SIDE * CAP, 1), F32),
        dma((13,)),
        dma((3,)),
        dma((3,)),
        dma((6, 2, 2, peers)),
        dma((6, 2, 2, peers)),
        dma((4, 2, 2, 2, peers)),
        dma((4, 2, 2, 2, peers)),
        dma((2,)),
        dma((2,)),
    ]
    out = jax.ShapeDtypeStruct((1, steps, rows, width), BF16)
    results = pl.pallas_call(
        functools.partial(relay_kernel, sections),
        out_shape=(out, out),
        in_specs=[in_hbm] * 13,
        out_specs=(in_vmem, in_vmem),
        scratch_shapes=scratch,
        compiler_params=pltpu.CompilerParams(
            collective_id=0, has_side_effects=True, vmem_limit_bytes=60 * 2**20
        ),
        name="relay",
    )(
        fwd_in,
        fwd_enter,
        bwd_in,
        bwd_enter,
        saved,
        *turned,
        gain,
        w_gate[0],
        w_up[0],
        w_down[0],
    )
    return pl.pallas_call(
        store_kernel,
        out_shape=(out, out),
        in_specs=[pl.BlockSpec(memory_space=pltpu.VMEM)] * 2,
        out_specs=(pl.BlockSpec(memory_space=pl.ANY),) * 2,
        scratch_shapes=[dma((2,))],
        name="store",
    )(*results)


def store_kernel(fwd, bwd, fwd_to, bwd_to, sems):
    copies = [
        pltpu.make_async_copy(source, target, sems.at[i])
        for i, (source, target) in enumerate(((fwd, fwd_to), (bwd, bwd_to)))
    ]
    for copy in copies:
        copy.start()
    for copy in copies:
        copy.wait()


def solution(mesh):
    in_specs = (
        P("section", "expert", None),
        P(None, "expert", None),
        P("section", "expert", None),
        P(None, "expert", None),
        P("section", None, "expert", None),
        P("section", None, None, None),
        P("section", None, None, None),
        P("section", None, None, None),
        P("section", None, None, None),
        P("section", None),
        P("section", None, "expert"),
        P("section", None, "expert"),
        P("section", "expert", None),
    )
    out_specs = (P("section", None, "expert", None), P("section", None, "expert", None))
    return jax.shard_map(
        per_device, mesh=mesh, in_specs=in_specs, out_specs=out_specs, check_vma=False
    )
```

```python
import functools

import jax
import jax.numpy as jnp
from jax import lax
from jax.experimental import pallas as pl
from jax.experimental.pallas import tpu as pltpu
from jax.sharding import PartitionSpec as P

EPSILON = 1e-06
MESH = pl.DeviceIdType.MESH
SIDE = 4
CORES = 2
PEERS = (2, 1, 3)
CAP = 6
F32 = jnp.float32
BF16 = jnp.bfloat16


def normalize(inputs, gain):
    scale = lax.rsqrt(jnp.mean(inputs * inputs, axis=-1, keepdims=True) + EPSILON)
    return scale, (inputs * scale * gain).astype(BF16)


def relay_kernel(
    sections,
    fwd_in,
    fwd_enter,
    bwd_in,
    bwd_enter,
    saved,
    fwd_routes,
    fwd_gates,
    bwd_routes,
    bwd_gates,
    gain,
    w_gate,
    w_up,
    w_down,
    fwd_out,
    bwd_out,
    in_f,
    enter_f,
    in_b,
    enter_b,
    in_s,
    routes_f,
    gates_f,
    routes_b,
    gates_b,
    gain_v,
    w_in,
    w_back,
    w_in_turned,
    line_y,
    line_x,
    packed_x,
    packed_y,
    outgoing,
    partial_x,
    partial_y,
    landed_x,
    landed_y,
    middle,
    landed_two,
    hop_send,
    hop_land,
    pre_act,
    pick_x,
    pick_y,
    weight_of,
    load_sem,
    weight_send,
    weight_recv,
    gather_send,
    gather_recv,
    reduce_send,
    reduce_recv,
    hop_send_sem,
    hop_recv_sem,
):
    width = gain.shape[-1]
    half = width // 2
    unit = w_down.shape[0]
    rows = in_f.shape[0]
    tokens = SIDE * SIDE * rows
    section = lax.axis_index("section")
    place = lax.axis_index("expert")
    core = lax.rem(place, CORES)
    x = lax.rem(place // CORES, SIDE)
    y = place // (CORES * SIDE)

    def device(dy=0, dx=0, dc=0, dz=0):
        at_y, at_x = lax.rem(y + dy, SIDE), lax.rem(x + dx, SIDE)
        at_c = lax.rem(core + dc, CORES)
        return (lax.rem(section + dz, sections), (at_y * SIDE + at_x) * CORES + at_c)

    sibling = device(dc=1)
    following, preceding = device(dz=1), device(dz=sections - 1)
    along_y = [device(dy=k) for k in PEERS]
    along_x = [device(dx=k) for k in PEERS]

    barrier = pltpu.get_barrier_semaphore()
    greeted = [sibling, following, preceding] + along_y + along_x
    for other in greeted:
        pl.semaphore_signal(barrier, inc=1, device_id=other, device_id_type=MESH)

    small = [
        (fwd_in.at[0], in_f),
        (gain, gain_v),
        (saved.at[0], in_s),
        (bwd_in.at[0], in_b),
        (fwd_routes, routes_f),
        (fwd_gates, gates_f),
        (bwd_routes, routes_b),
        (bwd_gates, gates_b),
        (fwd_enter.at[0], enter_f),
        (bwd_enter.at[0], enter_b),
    ]
    own_weights = [
        (w_gate, w_in.at[:, pl.ds(0, unit)]),
        (w_up, w_in.at[:, pl.ds(2 * unit, unit)]),
        (w_down, w_back.at[pl.ds(0, unit), :]),
    ]
    sibling_weights = [
        (w_gate, w_in.at[:, pl.ds(unit, unit)]),
        (w_up, w_in.at[:, pl.ds(3 * unit, unit)]),
        (w_down, w_back.at[pl.ds(unit, unit), :]),
    ]
    loads = [
        pltpu.make_async_copy(source, target, load_sem.at[i])
        for i, (source, target) in enumerate(small + own_weights)
    ]
    for load in loads:
        load.start()
    loads[1].wait()
    loads[2].wait()
    gain_row = gain_v[...]
    first, second = pl.ds(0, half), pl.ds(half, half)

    def place_own(u, block):
        line_y[u, y] = block[:, :half]
        line_x[u, x] = block[:, half:]

    scale, normed = normalize(in_s[0].astype(F32), gain_row)
    scales = [scale]
    place_own(1, normed)
    pl.semaphore_wait(barrier, len(greeted))

    sent = []

    def start(copies):
        for copy in copies:
            copy.start()
        sent.extend(copies)
        return copies

    def arrive(copies):
        for copy in copies:
            copy.wait_recv()

    def remote(source, target, send, recv, index, other):
        return pltpu.make_async_remote_copy(
            src_ref=source,
            dst_ref=target,
            send_sem=send.at[index],
            recv_sem=recv.at[index],
            device_id=other,
            device_id_type=MESH,
        )

    blocks = SIDE * SIDE * CORES
    slots = SIDE * CAP
    whole = SIDE * slots

    def iota(shape, axis):
        return lax.broadcasted_iota(jnp.int32, shape, axis)

    def choose():
        experts = iota((SIDE, blocks * rows), 0)
        hits, lines = [], []
        for routes, gates in ((routes_f, gates_f), (routes_b, gates_b)):
            for step in range(2):
                chosen = [routes[step, k : k + 1] == experts for k in range(2)]
                hits.append(jnp.where(chosen[0] | chosen[1], 1.0, 0.0))
                own = [jnp.where(routes[step, k : k + 1] == y, gates[step, k : k + 1], 0.0) for k in range(2)]
                lines.append(own[0] + own[1])
        hit = jnp.concatenate(hits, axis=0)
        from_lane, to_lane = (iota((blocks * rows, blocks * rows), axis) for axis in (0, 1))
        earlier = (from_lane // rows == to_lane // rows) & (from_lane < to_lane)
        rank = jnp.dot(
            hit.astype(BF16), jnp.where(earlier, 1.0, 0.0).astype(BF16), preferred_element_type=F32
        )
        key = jnp.where(hit > 0.5, rank, 64.0)
        lane, spot = iota((blocks * rows, SIDE * rows), 0), iota((blocks * rows, SIDE * rows), 1)
        near = lax.rem(spot, rows)
        in_column = lane == (((spot // rows) * SIDE + x) * CORES + core) * rows + near
        in_row = lane == ((y * SIDE + spot // rows) * CORES + core) * rows + near
        keys = [
            jnp.dot(
                key.astype(BF16), jnp.where(at, 1.0, 0.0).astype(BF16), preferred_element_type=F32
            )
            for at in (in_column, in_row)
        ]
        slot, spot = iota((slots, SIDE * rows), 0), iota((slots, SIDE * rows), 1)
        aligned = spot // rows == slot // CAP
        number = lax.rem(slot, CAP).astype(F32)
        order = iota((whole, blocks * rows), 0)
        lanes = iota((whole, blocks * rows), 1)
        block = (lax.rem(order // CAP, SIDE) * SIDE + order // slots) * CORES + core
        mine = lanes // rows == block
        position = lax.rem(order, CAP).astype(F32)
        is_own = iota((SIDE, SIDE * rows), 0) == y
        is_own_wide = iota((SIDE, blocks * rows), 0) == y
        for r in range(4):
            part = slice(r * SIDE, (r + 1) * SIDE)
            own = jnp.sum(jnp.where(is_own, keys[0][part], 0.0), axis=0, keepdims=True)
            pick_x[r] = jnp.where(aligned & (own == number), 1.0, 0.0)
            for e in range(SIDE):
                here = keys[1][r * SIDE + e : r * SIDE + e + 1]
                pick_y[r, e * slots : (e + 1) * slots] = jnp.where(
                    aligned & (here == number), 1.0, 0.0
                )
            own = jnp.sum(jnp.where(is_own_wide, key[part], 0.0), axis=0, keepdims=True)
            weight_of[r] = jnp.sum(
                jnp.where(mine & (own == position), lines[r], 0.0), axis=-1, keepdims=True
            )

    order, other = iota((whole, whole), 0), iota((whole, whole), 1)
    turned = lax.rem(order // CAP, SIDE) * slots + (order // slots) * CAP + lax.rem(order, CAP)
    turn = jnp.where(turned == other, 1.0, 0.0).astype(BF16)

    def gather_one(u):
        out = []
        for k in range(len(PEERS)):
            spot = line_y.at[u, y]
            out.append(remote(spot, spot, gather_send, gather_recv, (u, 0, 0, k), along_y[k]))
            spot = line_x.at[u, x]
            out.append(remote(spot, spot, gather_send, gather_recv, (u, 0, 1, k), along_x[k]))
        return out

    tiles = slots // rows

    def gather_two(u, r, ones):
        arrive(ones[0::2])
        block = line_y[u].reshape(SIDE * rows, half)
        packed = jnp.dot(pick_x[r].astype(BF16), block, preferred_element_type=F32)
        packed_x[u, x] = packed.astype(BF16).reshape(tiles, rows, half)
        spot = packed_x.at[u, x]
        across_x = start(
            [
                remote(spot, spot, gather_send, gather_recv, (u, 1, 0, k), along_x[k])
                for k in range(len(PEERS))
            ]
        )
        arrive(ones[1::2])
        block = line_x[u].reshape(SIDE * rows, half)
        packed = jnp.dot(pick_y[r].astype(BF16), block, preferred_element_type=F32)
        outgoing[u] = packed.astype(BF16).reshape(SIDE, tiles, rows, half)
        across_y = []
        for k, step in enumerate(PEERS):
            source, target = outgoing.at[u, lax.rem(y + step, SIDE)], packed_y.at[u, y]
            across_y.append(
                remote(source, target, gather_send, gather_recv, (u, 1, 1, k), along_y[k])
            )
        start(across_y)
        packed_y[u, y] = outgoing[u, y]
        return across_x, across_y

    def by_column(u):
        return packed_x[u].reshape(whole, half)

    def by_row(u):
        return turn_rows(packed_y[u].reshape(whole, half))

    def turn_rows(array):
        return jnp.dot(turn, array, preferred_element_type=F32).astype(BF16)

    def reduce_x(u):
        out = []
        for k, step in enumerate(PEERS):
            source, target = partial_x.at[u, lax.rem(x + step, SIDE)], landed_x.at[u, k]
            out.append(remote(source, target, reduce_send, reduce_recv, (u, 0, 0, k), along_x[k]))
        return start(out)

    def reduce_y(u):
        out = []
        for k, step in enumerate(PEERS):
            source, target = partial_y.at[u, lax.rem(y + step, SIDE)], landed_y.at[u, y]
            out.append(remote(source, target, reduce_send, reduce_recv, (u, 0, 1, k), along_y[k]))
        start(out)
        landed_y[u, y] = partial_y[u, y]
        return out

    transposed = (((0,), (0,)), ((), ()))

    def last_leg(u, part, at, peers):
        out = []
        for k, step in enumerate(PEERS):
            source, target = middle.at[u, part, lax.rem(at + step, SIDE)], landed_two.at[u, part, k]
            out.append(remote(source, target, reduce_send, reduce_recv, (u, 1, part, k), peers[k]))
        return start(out)

    def reduce_two(u, r, ones):
        arrive(ones[0])
        total = partial_x[u, x].astype(F32)
        for k in range(len(PEERS)):
            total = total + landed_x[u, k].astype(F32)
        spread = lax.dot_general(
            pick_x[r].astype(BF16),
            total.astype(BF16).reshape(slots, half),
            transposed,
            preferred_element_type=F32,
        )
        middle[u, 0] = spread.astype(BF16).reshape(SIDE, rows, half)
        across_y = last_leg(u, 0, y, along_y)
        arrive(ones[1])
        spread = lax.dot_general(
            pick_y[r].astype(BF16),
            landed_y[u].reshape(whole, half),
            transposed,
            preferred_element_type=F32,
        )
        middle[u, 1] = spread.astype(BF16).reshape(SIDE, rows, half)
        return across_y + last_leg(u, 1, x, along_x)

    def reduce_end(u):
        sums = []
        for part, at in enumerate((y, x)):
            total = middle[u, part, at].astype(F32)
            for k in range(len(PEERS)):
                total = total + landed_two[u, part, k].astype(F32)
            sums.append(total)
        return jnp.concatenate(sums, axis=-1)

    def pre_activation(u, twos):
        arrive(twos[0])
        both = jnp.dot(by_column(u), w_in[first, :], preferred_element_type=F32)
        arrive(twos[1])
        return both + jnp.dot(by_row(u), w_in[second, :], preferred_element_type=F32)

    shape = (SIDE, tiles, rows, half)

    def forward(target, r, both):
        a, up = both[:, : 2 * unit], both[:, 2 * unit :]
        hidden = (a / (1.0 + jnp.exp(-a)) * up * weight_of[r]).astype(BF16)
        piece = jnp.dot(hidden, w_back[:, first], preferred_element_type=F32)
        partial_x[target] = piece.astype(BF16).reshape(shape)
        across_x = reduce_x(target)
        piece = jnp.dot(turn_rows(hidden), w_back[:, second], preferred_element_type=F32)
        partial_y[target] = piece.astype(BF16).reshape(shape)
        return across_x, reduce_y(target)

    contract = (((1,), (1,)), ((), ()))

    def backward(u, target, both, r, twos):
        a, up = both[:, : 2 * unit], both[:, 2 * unit :]
        arrive(twos[0])
        d_hidden = lax.dot_general(
            by_column(u), w_back[:, first], contract, preferred_element_type=F32
        )
        arrive(twos[1])
        d_hidden = d_hidden + lax.dot_general(
            by_row(u), w_back[:, second], contract, preferred_element_type=F32
        )
        d_hidden = d_hidden * weight_of[r]
        sigma = 1.0 / (1.0 + jnp.exp(-a))
        d_gate = (d_hidden * up * sigma * (1.0 + a * (1.0 - sigma))).astype(BF16)
        d_up = (d_hidden * a * sigma).astype(BF16)
        grads = jnp.concatenate([d_gate, d_up], axis=-1)
        piece = jnp.dot(grads, w_in_turned[:, first], preferred_element_type=F32)
        partial_x[target] = piece.astype(BF16).reshape(shape)
        across_x = reduce_x(target)
        piece = jnp.dot(turn_rows(grads), w_in_turned[:, second], preferred_element_type=F32)
        partial_y[target] = piece.astype(BF16).reshape(shape)
        return across_x, reduce_y(target)

    def turn_weights():
        span = 2 * unit
        eye = jnp.where(iota((span, span), 0) == iota((span, span), 1), 1.0, 0.0).astype(BF16)
        for i in range(2):
            for rows_of in (first, second):
                turned_part = lax.dot_general(
                    eye,
                    w_in[rows_of, pl.ds(i * span, span)],
                    contract,
                    preferred_element_type=F32,
                )
                w_in_turned[pl.ds(i * span, span), rows_of] = turned_part.astype(BF16)

    def forward_end(u, inputs):
        return (inputs.astype(F32) + reduce_end(u)).astype(BF16)

    def backward_end(u, step, upstream):
        inputs = in_s[step].astype(F32)
        scale = scales[step]
        product = reduce_end(u) * gain_row
        change = scale * product - inputs * scale**3 * jnp.mean(
            product * inputs, axis=-1, keepdims=True
        )
        return (upstream.astype(F32) + change).astype(BF16)

    def hop(i, block, other):
        hop_send[i] = block
        return start(
            [remote(hop_send.at[i], hop_land.at[i], hop_send_sem, hop_recv_sem, (i,), other)]
        )

    for load in [loads[0]] + loads[3 : len(small)]:
        load.wait()
    place_own(2, in_b[...])
    gather_s = start(gather_one(1))
    gather_g = start(gather_one(2))
    weights = [
        remote(source, target, weight_send, weight_recv, (i,), sibling)
        for i, (source, target) in enumerate(sibling_weights)
    ]
    start(weights)
    _, normed = normalize(in_f[...].astype(F32), gain_row)
    place_own(0, normed)
    gather_f = start(gather_one(0))
    scale, normed = normalize(in_s[1].astype(F32), gain_row)
    scales.append(scale)
    place_own(4, normed)
    choose()
    gather_s = gather_two(1, 2, gather_s)
    gather_g = gather_two(2, 2, gather_g)
    gather_f = gather_two(0, 0, gather_f)
    gather_n = start(gather_one(4))
    for load in loads[len(small) :]:
        load.wait()
    arrive(weights)
    turn_weights()
    both = pre_activation(1, gather_s)
    reduce_b = backward(2, 1, both, 2, gather_g)
    both = pre_activation(0, gather_f)
    reduce_f = forward(0, 0, both)
    reduce_b = reduce_two(1, 2, reduce_b)
    reduce_f = reduce_two(0, 0, reduce_f)
    gather_n = gather_two(4, 3, gather_n)
    arrive(reduce_b)
    outputs = backward_end(1, 0, in_b[...])
    hop_b = hop(1, outputs, preceding)
    arrive(reduce_f)
    outputs = forward_end(0, in_f[...])
    hop_f = hop(0, outputs, following)
    bwd_out[0, 0] = hop_send[1]
    fwd_out[0, 0] = hop_send[0]

    arrive(hop_b)
    moved_b = jnp.where(
        section == sections - 1, enter_b[...].astype(F32), hop_land[1].astype(F32)
    ).astype(BF16)
    place_own(5, moved_b)
    gather_g = start(gather_one(5))
    arrive(hop_f)
    moved_f = jnp.where(section == 0, enter_f[...].astype(F32), hop_land[0].astype(F32))
    _, normed = normalize(moved_f, gain_row)
    place_own(3, normed)
    gather_f = start(gather_one(3))
    gather_g = gather_two(5, 3, gather_g)
    pre_act[...] = pre_activation(4, gather_n)
    gather_f = gather_two(3, 1, gather_f)
    reduce_b = backward(5, 3, pre_act[...], 3, gather_g)
    both = pre_activation(3, gather_f)
    reduce_f = forward(2, 1, both)
    reduce_b = reduce_two(3, 3, reduce_b)
    reduce_f = reduce_two(2, 1, reduce_f)
    arrive(reduce_b)
    bwd_out[0, 1] = backward_end(3, 1, moved_b)
    arrive(reduce_f)
    fwd_out[0, 1] = forward_end(2, moved_f)
    for copy in sent:
        copy.wait_send()


def per_device(
    fwd_in,
    fwd_enter,
    bwd_in,
    bwd_enter,
    saved,
    fwd_routes,
    fwd_gates,
    bwd_routes,
    bwd_gates,
    gain,
    w_gate,
    w_up,
    w_down,
):
    sections = lax.axis_size("section")
    steps, rows, width = saved.shape[1:]
    unit = w_gate.shape[-1]
    half = width // 2
    peers = len(PEERS)
    tiles = SIDE * CAP // rows
    turned = [
        jnp.transpose(array[0], (0, 2, 1)) for array in (fwd_routes, fwd_gates, bwd_routes, bwd_gates)
    ]
    in_hbm = pl.BlockSpec(memory_space=pltpu.HBM)
    in_vmem = pl.BlockSpec(memory_space=pltpu.VMEM)
    table = turned[0].shape
    dma = pltpu.SemaphoreType.DMA
    scratch = [
        pltpu.VMEM((rows, width), BF16),
        pltpu.VMEM((rows, width), BF16),
        pltpu.VMEM((rows, width), BF16),
        pltpu.VMEM((rows, width), BF16),
        pltpu.VMEM((steps, rows, width), BF16),
        pltpu.VMEM(table, jnp.int32),
        pltpu.VMEM(table, F32),
        pltpu.VMEM(table, jnp.int32),
        pltpu.VMEM(table, F32),
        pltpu.VMEM((1, width), F32),
        pltpu.VMEM((width, 4 * unit), BF16),
        pltpu.VMEM((2 * unit, width), BF16),
        pltpu.VMEM((4 * unit, width), BF16),
        pltpu.VMEM((6, SIDE, rows, half), BF16),
        pltpu.VMEM((6, SIDE, rows, half), BF16),
        pltpu.VMEM((6, SIDE, tiles, rows, half), BF16),
        pltpu.VMEM((6, SIDE, tiles, rows, half), BF16),
        pltpu.VMEM((6, SIDE, tiles, rows, half), BF16),
        pltpu.VMEM((4, SIDE, tiles, rows, half), BF16),
        pltpu.VMEM((4, SIDE, tiles, rows, half), BF16),
        pltpu.VMEM((4, peers, tiles, rows, half), BF16),
        pltpu.VMEM((4, SIDE, tiles, rows, half), BF16),
        pltpu.VMEM((4, 2, SIDE, rows, half), BF16),
        pltpu.VMEM((4, 2, peers, rows, half), BF16),
        pltpu.VMEM((2, rows, width), BF16),
        pltpu.VMEM((2, rows, width), BF16),
        pltpu.VMEM((SIDE * SIDE * CAP, 4 * unit), F32),
        pltpu.VMEM((4, SIDE * CAP, SIDE * rows), F32),
        pltpu.VMEM((4, SIDE * SIDE * CAP, SIDE * rows), F32),
        pltpu.VMEM((4, SIDE * SIDE * CAP, 1), F32),
        dma((13,)),
        dma((3,)),
        dma((3,)),
        dma((6, 2, 2, peers)),
        dma((6, 2, 2, peers)),
        dma((4, 2, 2, peers)),
        dma((4, 2, 2, peers)),
        dma((2,)),
        dma((2,)),
    ]
    out = jax.ShapeDtypeStruct((1, steps, rows, width), BF16)
    results = pl.pallas_call(
        functools.partial(relay_kernel, sections),
        out_shape=(out, out),
        in_specs=[in_hbm] * 13,
        out_specs=(in_vmem, in_vmem),
        scratch_shapes=scratch,
        compiler_params=pltpu.CompilerParams(
            collective_id=0, has_side_effects=True, vmem_limit_bytes=60 * 2**20
        ),
        name="relay",
    )(
        fwd_in,
        fwd_enter,
        bwd_in,
        bwd_enter,
        saved,
        *turned,
        gain,
        w_gate[0],
        w_up[0],
        w_down[0],
    )
    return pl.pallas_call(
        store_kernel,
        out_shape=(out, out),
        in_specs=[pl.BlockSpec(memory_space=pltpu.VMEM)] * 2,
        out_specs=(pl.BlockSpec(memory_space=pl.ANY),) * 2,
        scratch_shapes=[dma((2,))],
        name="store",
    )(*results)


def store_kernel(fwd, bwd, fwd_to, bwd_to, sems):
    copies = [
        pltpu.make_async_copy(source, target, sems.at[i])
        for i, (source, target) in enumerate(((fwd, fwd_to), (bwd, bwd_to)))
    ]
    for copy in copies:
        copy.start()
    for copy in copies:
        copy.wait()


def solution(mesh):
    in_specs = (
        P("section", "expert", None),
        P(None, "expert", None),
        P("section", "expert", None),
        P(None, "expert", None),
        P("section", None, "expert", None),
        P("section", None, None, None),
        P("section", None, None, None),
        P("section", None, None, None),
        P("section", None, None, None),
        P("section", None),
        P("section", None, "expert"),
        P("section", None, "expert"),
        P("section", "expert", None),
    )
    out_specs = (P("section", None, "expert", None), P("section", None, "expert", None))
    return jax.shard_map(
        per_device, mesh=mesh, in_specs=in_specs, out_specs=out_specs, check_vma=False
    )
```

```python
import functools

import jax
import jax.numpy as jnp
from jax import lax
from jax.experimental import pallas as pl
from jax.experimental.pallas import tpu as pltpu
from jax.sharding import PartitionSpec as P

EPSILON = 1e-06
MESH = pl.DeviceIdType.MESH
SIDE = 4
CORES = 2
PEERS = (2, 1, 3)
CAP = 6
F32 = jnp.float32
BF16 = jnp.bfloat16


def normalize(inputs, gain):
    scale = lax.rsqrt(jnp.mean(inputs * inputs, axis=-1, keepdims=True) + EPSILON)
    return scale, (inputs * scale * gain).astype(BF16)


def relay_kernel(
    sections,
    fwd_in,
    fwd_enter,
    bwd_in,
    bwd_enter,
    saved,
    fwd_routes,
    fwd_gates,
    bwd_routes,
    bwd_gates,
    gain,
    w_gate,
    w_up,
    w_down,
    fwd_out,
    bwd_out,
    in_f,
    enter_f,
    in_b,
    enter_b,
    in_s,
    routes_f,
    gates_f,
    routes_b,
    gates_b,
    gain_v,
    w_in,
    w_back,
    w_in_turned,
    line_y,
    line_x,
    packed_x,
    packed_y,
    outgoing,
    partial_x,
    partial_y,
    landed_x,
    landed_y,
    middle,
    landed_two,
    hop_send,
    hop_land,
    pre_act,
    pick_x,
    pick_y,
    weight_of,
    load_sem,
    weight_send,
    weight_recv,
    gather_send,
    gather_recv,
    reduce_send,
    reduce_recv,
    hop_send_sem,
    hop_recv_sem,
):
    width = gain.shape[-1]
    half = width // 2
    unit = w_down.shape[0]
    rows = in_f.shape[0]
    tokens = SIDE * SIDE * rows
    section = lax.axis_index("section")
    place = lax.axis_index("expert")
    core = lax.rem(place, CORES)
    x = lax.rem(place // CORES, SIDE)
    y = place // (CORES * SIDE)

    def device(dy=0, dx=0, dc=0, dz=0):
        at_y, at_x = lax.rem(y + dy, SIDE), lax.rem(x + dx, SIDE)
        at_c = lax.rem(core + dc, CORES)
        return (lax.rem(section + dz, sections), (at_y * SIDE + at_x) * CORES + at_c)

    sibling = device(dc=1)
    following, preceding = device(dz=1), device(dz=sections - 1)
    along_y = [device(dy=k) for k in PEERS]
    along_x = [device(dx=k) for k in PEERS]

    barrier = pltpu.get_barrier_semaphore()
    greeted = [sibling, following, preceding] + along_y + along_x
    for other in greeted:
        pl.semaphore_signal(barrier, inc=1, device_id=other, device_id_type=MESH)

    small = [
        (fwd_in.at[0], in_f),
        (gain, gain_v),
        (saved.at[0], in_s),
        (bwd_in.at[0], in_b),
        (fwd_routes, routes_f),
        (fwd_gates, gates_f),
        (bwd_routes, routes_b),
        (bwd_gates, gates_b),
        (fwd_enter.at[0], enter_f),
        (bwd_enter.at[0], enter_b),
    ]
    own_weights = [
        (w_gate, w_in.at[:, pl.ds(0, unit)]),
        (w_up, w_in.at[:, pl.ds(2 * unit, unit)]),
        (w_down, w_back.at[pl.ds(0, unit), :]),
    ]
    sibling_weights = [
        (w_gate, w_in.at[:, pl.ds(unit, unit)]),
        (w_up, w_in.at[:, pl.ds(3 * unit, unit)]),
        (w_down, w_back.at[pl.ds(unit, unit), :]),
    ]
    loads = [
        pltpu.make_async_copy(source, target, load_sem.at[i])
        for i, (source, target) in enumerate(small + own_weights)
    ]
    for load in loads:
        load.start()
    loads[1].wait()
    loads[2].wait()
    gain_row = gain_v[...]
    first, second = pl.ds(0, half), pl.ds(half, half)

    def place_own(u, block):
        line_y[u, y] = block[:, :half]
        line_x[u, x] = block[:, half:]

    scale, normed = normalize(in_s[0].astype(F32), gain_row)
    scales = [scale]
    place_own(1, normed)
    pl.semaphore_wait(barrier, len(greeted))

    sent = []

    def start(copies):
        for copy in copies:
            copy.start()
        sent.extend(copies)
        return copies

    def arrive(copies):
        for copy in copies:
            copy.wait_recv()

    def remote(source, target, send, recv, index, other):
        return pltpu.make_async_remote_copy(
            src_ref=source,
            dst_ref=target,
            send_sem=send.at[index],
            recv_sem=recv.at[index],
            device_id=other,
            device_id_type=MESH,
        )

    blocks = SIDE * SIDE * CORES
    slots = SIDE * CAP
    whole = SIDE * slots

    def iota(shape, axis):
        return lax.broadcasted_iota(jnp.int32, shape, axis)

    def choose():
        experts = iota((SIDE, blocks * rows), 0)
        hits, lines = [], []
        for routes, gates in ((routes_f, gates_f), (routes_b, gates_b)):
            for step in range(2):
                chosen = [routes[step, k : k + 1] == experts for k in range(2)]
                hits.append(jnp.where(chosen[0] | chosen[1], 1.0, 0.0))
                own = [jnp.where(routes[step, k : k + 1] == y, gates[step, k : k + 1], 0.0) for k in range(2)]
                lines.append(own[0] + own[1])
        hit = jnp.concatenate(hits, axis=0)
        from_lane, to_lane = (iota((blocks * rows, blocks * rows), axis) for axis in (0, 1))
        earlier = (from_lane // rows == to_lane // rows) & (from_lane < to_lane)
        rank = jnp.dot(
            hit.astype(BF16), jnp.where(earlier, 1.0, 0.0).astype(BF16), preferred_element_type=F32
        )
        key = jnp.where(hit > 0.5, rank, 64.0)
        lane, spot = iota((blocks * rows, SIDE * rows), 0), iota((blocks * rows, SIDE * rows), 1)
        near = lax.rem(spot, rows)
        in_column = lane == (((spot // rows) * SIDE + x) * CORES + core) * rows + near
        in_row = lane == ((y * SIDE + spot // rows) * CORES + core) * rows + near
        keys = [
            jnp.dot(
                key.astype(BF16), jnp.where(at, 1.0, 0.0).astype(BF16), preferred_element_type=F32
            )
            for at in (in_column, in_row)
        ]
        slot, spot = iota((slots, SIDE * rows), 0), iota((slots, SIDE * rows), 1)
        aligned = spot // rows == slot // CAP
        number = lax.rem(slot, CAP).astype(F32)
        order = iota((whole, blocks * rows), 0)
        lanes = iota((whole, blocks * rows), 1)
        block = (lax.rem(order // CAP, SIDE) * SIDE + order // slots) * CORES + core
        mine = lanes // rows == block
        position = lax.rem(order, CAP).astype(F32)
        is_own = iota((SIDE, SIDE * rows), 0) == y
        is_own_wide = iota((SIDE, blocks * rows), 0) == y
        for r in range(4):
            part = slice(r * SIDE, (r + 1) * SIDE)
            own = jnp.sum(jnp.where(is_own, keys[0][part], 0.0), axis=0, keepdims=True)
            pick_x[r] = jnp.where(aligned & (own == number), 1.0, 0.0)
            for e in range(SIDE):
                here = keys[1][r * SIDE + e : r * SIDE + e + 1]
                pick_y[r, e * slots : (e + 1) * slots] = jnp.where(
                    aligned & (here == number), 1.0, 0.0
                )
            own = jnp.sum(jnp.where(is_own_wide, key[part], 0.0), axis=0, keepdims=True)
            weight_of[r] = jnp.sum(
                jnp.where(mine & (own == position), lines[r], 0.0), axis=-1, keepdims=True
            )

    order, other = iota((whole, whole), 0), iota((whole, whole), 1)
    turned = lax.rem(order // CAP, SIDE) * slots + (order // slots) * CAP + lax.rem(order, CAP)
    turn = jnp.where(turned == other, 1.0, 0.0).astype(BF16)

    def gather_one(u):
        out = []
        for k in range(len(PEERS)):
            spot = line_y.at[u, y]
            out.append(remote(spot, spot, gather_send, gather_recv, (u, 0, 0, k), along_y[k]))
            spot = line_x.at[u, x]
            out.append(remote(spot, spot, gather_send, gather_recv, (u, 0, 1, k), along_x[k]))
        return out

    tiles = slots // rows

    def gather_two(u, r, ones):
        arrive(ones[0::2])
        block = line_y[u].reshape(SIDE * rows, half)
        packed = jnp.dot(pick_x[r].astype(BF16), block, preferred_element_type=F32)
        packed_x[u, x] = packed.astype(BF16).reshape(tiles, rows, half)
        spot = packed_x.at[u, x]
        across_x = start(
            [
                remote(spot, spot, gather_send, gather_recv, (u, 1, 0, k), along_x[k])
                for k in range(len(PEERS))
            ]
        )
        arrive(ones[1::2])
        block = line_x[u].reshape(SIDE * rows, half)
        packed = jnp.dot(pick_y[r].astype(BF16), block, preferred_element_type=F32)
        outgoing[u] = packed.astype(BF16).reshape(SIDE, tiles, rows, half)
        across_y = []
        for k, step in enumerate(PEERS):
            source, target = outgoing.at[u, lax.rem(y + step, SIDE)], packed_y.at[u, y]
            across_y.append(
                remote(source, target, gather_send, gather_recv, (u, 1, 1, k), along_y[k])
            )
        start(across_y)
        packed_y[u, y] = outgoing[u, y]
        return across_x, across_y

    def by_column(u):
        return packed_x[u].reshape(whole, half)

    def by_row(u):
        return turn_rows(packed_y[u].reshape(whole, half))

    def turn_rows(array):
        return jnp.dot(turn, array, preferred_element_type=F32).astype(BF16)

    def reduce_x(u):
        out = []
        for k, step in enumerate(PEERS):
            source, target = partial_x.at[u, lax.rem(x + step, SIDE)], landed_x.at[u, k]
            out.append(remote(source, target, reduce_send, reduce_recv, (u, 0, 0, k), along_x[k]))
        return start(out)

    def reduce_y(u):
        out = []
        for k, step in enumerate(PEERS):
            source, target = partial_y.at[u, lax.rem(y + step, SIDE)], landed_y.at[u, y]
            out.append(remote(source, target, reduce_send, reduce_recv, (u, 0, 1, k), along_y[k]))
        start(out)
        landed_y[u, y] = partial_y[u, y]
        return out

    transposed = (((0,), (0,)), ((), ()))

    def last_leg(u, part, at, peers):
        out = []
        for k, step in enumerate(PEERS):
            source, target = middle.at[u, part, lax.rem(at + step, SIDE)], landed_two.at[u, part, k]
            out.append(remote(source, target, reduce_send, reduce_recv, (u, 1, part, k), peers[k]))
        return start(out)

    def reduce_two(u, r, ones):
        arrive(ones[0])
        total = partial_x[u, x].astype(F32)
        for k in range(len(PEERS)):
            total = total + landed_x[u, k].astype(F32)
        spread = lax.dot_general(
            pick_x[r].astype(BF16),
            total.astype(BF16).reshape(slots, half),
            transposed,
            preferred_element_type=F32,
        )
        middle[u, 0] = spread.astype(BF16).reshape(SIDE, rows, half)
        across_y = last_leg(u, 0, y, along_y)
        arrive(ones[1])
        spread = lax.dot_general(
            pick_y[r].astype(BF16),
            landed_y[u].reshape(whole, half),
            transposed,
            preferred_element_type=F32,
        )
        middle[u, 1] = spread.astype(BF16).reshape(SIDE, rows, half)
        return across_y + last_leg(u, 1, x, along_x)

    def reduce_end(u):
        sums = []
        for part, at in enumerate((y, x)):
            total = middle[u, part, at].astype(F32)
            for k in range(len(PEERS)):
                total = total + landed_two[u, part, k].astype(F32)
            sums.append(total)
        return jnp.concatenate(sums, axis=-1)

    def pre_activation(u, twos):
        arrive(twos[0])
        both = jnp.dot(by_column(u), w_in[first, :], preferred_element_type=F32)
        arrive(twos[1])
        return both + jnp.dot(by_row(u), w_in[second, :], preferred_element_type=F32)

    shape = (SIDE, tiles, rows, half)

    def forward(target, r, both):
        a, up = both[:, : 2 * unit], both[:, 2 * unit :]
        hidden = (a / (1.0 + jnp.exp(-a)) * up * weight_of[r]).astype(BF16)
        piece = jnp.dot(hidden, w_back[:, first], preferred_element_type=F32)
        partial_x[target] = piece.astype(BF16).reshape(shape)
        across_x = reduce_x(target)
        piece = jnp.dot(turn_rows(hidden), w_back[:, second], preferred_element_type=F32)
        partial_y[target] = piece.astype(BF16).reshape(shape)
        return across_x, reduce_y(target)

    contract = (((1,), (1,)), ((), ()))

    def backward(u, target, both, r, twos):
        a, up = both[:, : 2 * unit], both[:, 2 * unit :]
        arrive(twos[0])
        d_hidden = lax.dot_general(
            by_column(u), w_back[:, first], contract, preferred_element_type=F32
        )
        arrive(twos[1])
        d_hidden = d_hidden + lax.dot_general(
            by_row(u), w_back[:, second], contract, preferred_element_type=F32
        )
        d_hidden = d_hidden * weight_of[r]
        sigma = 1.0 / (1.0 + jnp.exp(-a))
        d_gate = (d_hidden * up * sigma * (1.0 + a * (1.0 - sigma))).astype(BF16)
        d_up = (d_hidden * a * sigma).astype(BF16)
        grads = jnp.concatenate([d_gate, d_up], axis=-1)
        piece = jnp.dot(grads, w_in_turned[:, first], preferred_element_type=F32)
        partial_x[target] = piece.astype(BF16).reshape(shape)
        across_x = reduce_x(target)
        piece = jnp.dot(turn_rows(grads), w_in_turned[:, second], preferred_element_type=F32)
        partial_y[target] = piece.astype(BF16).reshape(shape)
        return across_x, reduce_y(target)

    def turn_weights():
        span = 2 * unit
        eye = jnp.where(iota((span, span), 0) == iota((span, span), 1), 1.0, 0.0).astype(BF16)
        for i in range(2):
            for rows_of in (first, second):
                turned_part = lax.dot_general(
                    eye,
                    w_in[rows_of, pl.ds(i * span, span)],
                    contract,
                    preferred_element_type=F32,
                )
                w_in_turned[pl.ds(i * span, span), rows_of] = turned_part.astype(BF16)

    def forward_end(u, inputs):
        return (inputs.astype(F32) + reduce_end(u)).astype(BF16)

    def backward_end(u, step, upstream):
        inputs = in_s[step].astype(F32)
        scale = scales[step]
        product = reduce_end(u) * gain_row
        change = scale * product - inputs * scale**3 * jnp.mean(
            product * inputs, axis=-1, keepdims=True
        )
        return (upstream.astype(F32) + change).astype(BF16)

    def hop(i, block, other):
        hop_send[i] = block
        return start(
            [remote(hop_send.at[i], hop_land.at[i], hop_send_sem, hop_recv_sem, (i,), other)]
        )

    for load in [loads[0]] + loads[3 : len(small)]:
        load.wait()
    place_own(2, in_b[...])
    gather_s = start(gather_one(1))
    gather_g = start(gather_one(2))
    weights = [
        remote(source, target, weight_send, weight_recv, (i,), sibling)
        for i, (source, target) in enumerate(sibling_weights)
    ]
    start(weights)
    _, normed = normalize(in_f[...].astype(F32), gain_row)
    place_own(0, normed)
    gather_f = start(gather_one(0))
    scale, normed = normalize(in_s[1].astype(F32), gain_row)
    scales.append(scale)
    place_own(4, normed)
    choose()
    gather_s = gather_two(1, 2, gather_s)
    gather_g = gather_two(2, 2, gather_g)
    gather_f = gather_two(0, 0, gather_f)
    gather_n = start(gather_one(4))
    for load in loads[len(small) :]:
        load.wait()
    arrive(weights)
    turn_weights()
    both = pre_activation(1, gather_s)
    reduce_b = backward(2, 1, both, 2, gather_g)
    both = pre_activation(0, gather_f)
    reduce_f = forward(0, 0, both)
    reduce_b = reduce_two(1, 2, reduce_b)
    reduce_f = reduce_two(0, 0, reduce_f)
    gather_n = gather_two(4, 3, gather_n)
    arrive(reduce_b)
    outputs = backward_end(1, 0, in_b[...])
    hop_b = hop(1, outputs, preceding)
    arrive(reduce_f)
    outputs = forward_end(0, in_f[...])
    hop_f = hop(0, outputs, following)
    bwd_out[0, 0] = hop_send[1]
    fwd_out[0, 0] = hop_send[0]

    arrive(hop_b)
    moved_b = jnp.where(
        section == sections - 1, enter_b[...].astype(F32), hop_land[1].astype(F32)
    ).astype(BF16)
    place_own(5, moved_b)
    gather_g = start(gather_one(5))
    arrive(hop_f)
    moved_f = jnp.where(section == 0, enter_f[...].astype(F32), hop_land[0].astype(F32))
    _, normed = normalize(moved_f, gain_row)
    place_own(3, normed)
    gather_f = start(gather_one(3))
    done = list(sent)
    sent.clear()
    gather_g = gather_two(5, 3, gather_g)
    pre_act[...] = pre_activation(4, gather_n)
    gather_f = gather_two(3, 1, gather_f)
    for copy in done:
        copy.wait_send()
    reduce_b = backward(5, 3, pre_act[...], 3, gather_g)
    both = pre_activation(3, gather_f)
    reduce_f = forward(2, 1, both)
    reduce_b = reduce_two(3, 3, reduce_b)
    reduce_f = reduce_two(2, 1, reduce_f)
    arrive(reduce_b)
    bwd_out[0, 1] = backward_end(3, 1, moved_b)
    arrive(reduce_f)
    fwd_out[0, 1] = forward_end(2, moved_f)
    for copy in sent:
        copy.wait_send()


def per_device(
    fwd_in,
    fwd_enter,
    bwd_in,
    bwd_enter,
    saved,
    fwd_routes,
    fwd_gates,
    bwd_routes,
    bwd_gates,
    gain,
    w_gate,
    w_up,
    w_down,
):
    sections = lax.axis_size("section")
    steps, rows, width = saved.shape[1:]
    unit = w_gate.shape[-1]
    half = width // 2
    peers = len(PEERS)
    tiles = SIDE * CAP // rows
    turned = [
        jnp.transpose(array[0], (0, 2, 1)) for array in (fwd_routes, fwd_gates, bwd_routes, bwd_gates)
    ]
    in_hbm = pl.BlockSpec(memory_space=pltpu.HBM)
    in_vmem = pl.BlockSpec(memory_space=pltpu.VMEM)
    table = turned[0].shape
    dma = pltpu.SemaphoreType.DMA
    scratch = [
        pltpu.VMEM((rows, width), BF16),
        pltpu.VMEM((rows, width), BF16),
        pltpu.VMEM((rows, width), BF16),
        pltpu.VMEM((rows, width), BF16),
        pltpu.VMEM((steps, rows, width), BF16),
        pltpu.VMEM(table, jnp.int32),
        pltpu.VMEM(table, F32),
        pltpu.VMEM(table, jnp.int32),
        pltpu.VMEM(table, F32),
        pltpu.VMEM((1, width), F32),
        pltpu.VMEM((width, 4 * unit), BF16),
        pltpu.VMEM((2 * unit, width), BF16),
        pltpu.VMEM((4 * unit, width), BF16),
        pltpu.VMEM((6, SIDE, rows, half), BF16),
        pltpu.VMEM((6, SIDE, rows, half), BF16),
        pltpu.VMEM((6, SIDE, tiles, rows, half), BF16),
        pltpu.VMEM((6, SIDE, tiles, rows, half), BF16),
        pltpu.VMEM((6, SIDE, tiles, rows, half), BF16),
        pltpu.VMEM((4, SIDE, tiles, rows, half), BF16),
        pltpu.VMEM((4, SIDE, tiles, rows, half), BF16),
        pltpu.VMEM((4, peers, tiles, rows, half), BF16),
        pltpu.VMEM((4, SIDE, tiles, rows, half), BF16),
        pltpu.VMEM((4, 2, SIDE, rows, half), BF16),
        pltpu.VMEM((4, 2, peers, rows, half), BF16),
        pltpu.VMEM((2, rows, width), BF16),
        pltpu.VMEM((2, rows, width), BF16),
        pltpu.VMEM((SIDE * SIDE * CAP, 4 * unit), F32),
        pltpu.VMEM((4, SIDE * CAP, SIDE * rows), F32),
        pltpu.VMEM((4, SIDE * SIDE * CAP, SIDE * rows), F32),
        pltpu.VMEM((4, SIDE * SIDE * CAP, 1), F32),
        dma((13,)),
        dma((3,)),
        dma((3,)),
        dma((6, 2, 2, peers)),
        dma((6, 2, 2, peers)),
        dma((4, 2, 2, peers)),
        dma((4, 2, 2, peers)),
        dma((2,)),
        dma((2,)),
    ]
    out = jax.ShapeDtypeStruct((1, steps, rows, width), BF16)
    results = pl.pallas_call(
        functools.partial(relay_kernel, sections),
        out_shape=(out, out),
        in_specs=[in_hbm] * 13,
        out_specs=(in_vmem, in_vmem),
        scratch_shapes=scratch,
        compiler_params=pltpu.CompilerParams(
            collective_id=0, has_side_effects=True, vmem_limit_bytes=60 * 2**20
        ),
        name="relay",
    )(
        fwd_in,
        fwd_enter,
        bwd_in,
        bwd_enter,
        saved,
        *turned,
        gain,
        w_gate[0],
        w_up[0],
        w_down[0],
    )
    return pl.pallas_call(
        store_kernel,
        out_shape=(out, out),
        in_specs=[pl.BlockSpec(memory_space=pltpu.VMEM)] * 2,
        out_specs=(pl.BlockSpec(memory_space=pl.ANY),) * 2,
        scratch_shapes=[dma((2,))],
        name="store",
    )(*results)


def store_kernel(fwd, bwd, fwd_to, bwd_to, sems):
    copies = [
        pltpu.make_async_copy(source, target, sems.at[i])
        for i, (source, target) in enumerate(((fwd, fwd_to), (bwd, bwd_to)))
    ]
    for copy in copies:
        copy.start()
    for copy in copies:
        copy.wait()


def solution(mesh):
    in_specs = (
        P("section", "expert", None),
        P(None, "expert", None),
        P("section", "expert", None),
        P(None, "expert", None),
        P("section", None, "expert", None),
        P("section", None, None, None),
        P("section", None, None, None),
        P("section", None, None, None),
        P("section", None, None, None),
        P("section", None),
        P("section", None, "expert"),
        P("section", None, "expert"),
        P("section", "expert", None),
    )
    out_specs = (P("section", None, "expert", None), P("section", None, "expert", None))
    return jax.shard_map(
        per_device, mesh=mesh, in_specs=in_specs, out_specs=out_specs, check_vma=False
    )
```
